128 devices in a mesh: shard: 16 (over z, x_lo, core), ctx: 8 (over x_hi, y).
Axes of the slice: x: 4 (x_hi: 2, x_lo: 2; x = x_hi * 2 + x_lo), y: 4, z: 4, core: 2. Of those that a mesh axis runs over, the one named last changes fastest.
Arguments:
- hidden_in: bfloat16 [32, 1024, 1024], P('shard', 'ctx'), may hold values from -6 to 6
- routes: int32 [32, 1024, 8], P('shard', 'ctx'), may hold values from 0 to 31, all different within a row; in each aligned block of 128 rows (0 to 127, 128 to 255, ..., all dimensions but the last counted through in order) at most 48 rows name the same one
- prefix: int32 [32], P('shard'), may hold values from 102 to 512
- gain_attention: bfloat16 [1024], P('shard'), may hold values from 0.5 to 1.5
- w_query: bfloat16 [1024, 1024], P('shard'), may hold values from -0.1875 to 0.1875
- w_keyval: bfloat16 [1024, 1024], P('shard'), may hold values from -0.1875 to 0.1875
- gain_query: bfloat16 [1024], P('shard'), may hold values from 0.5 to 1.5
- gain_key: bfloat16 [512], P('shard'), may hold values from 0.5 to 1.5
- w_output: bfloat16 [1024, 1024], P('shard'), may hold values from -3 to 3
- gain_experts: bfloat16 [1024], P('shard'), may hold values from 0.5 to 1.5
- w_router: bfloat16 [1024, 32], P('shard'), may hold values from -0.09375 to 0.09375
- w_gate_up: bfloat16 [32, 1024, 1024], P('shard', 'ctx'), may hold values from -0.1875 to 0.1875
- w_down: bfloat16 [32, 512, 1024], P('shard', None, 'ctx'), may hold values from -1 to 1
- cotangent: bfloat16 [32, 1024, 1024], P('shard', 'ctx'), may hold values from -6 to 6
Outputs:
- layer_out: bfloat16 [32, 1024, 1024], P('shard', 'ctx')
- grad_input: bfloat16 [32, 1024, 1024], P('shard', 'ctx')
- grad_gain_attention: float32 [1024], P('shard')
- query_weight_gradient: float32 [1024, 1024], P('shard')
- grad_w_keyval: float32 [1024, 1024], P('shard')
- grad_gain_query: float32 [1024], P('shard')
- grad_gain_key: float32 [512], P('shard')
- grad_w_output: float32 [1024, 1024], P('shard')
- grad_gain_experts: float32 [1024], P('shard')
- grad_w_router: float32 [1024, 32], P('shard')
- grad_w_gate_up: float32 [32, 1024, 1024], P('shard', 'ctx')
- grad_w_down: float32 [32, 512, 1024], P('shard', None, 'ctx')
The draws below stay inside these ranges and needn't reach their ends.
Inputs may be any that keep to these rules, and one draw needn't show every extreme that they name: `routes`: in each aligned block of 128 positions of a sequence, at most 48 tokens name one expert; a token names 8 different experts.
All inputs are finite; a program needn't handle non-finite values.
Results may differ from the reference program's by a relative error of at most 0.028.
Values may be sent and summed in bfloat16 or wider, within the bound.
No kernel may reach another device: no remote copies, remote signals or barrier semaphores. Data moves between devices by JAX's collectives and lax.ppermute only.
A program may use at most 256 MiB of HBM per device.

```python
import math
import jax
import jax.numpy as jnp
import numpy as np
from jax import lax

D = 1024
H = 16
KVH = 8
HD = 64
FF = 512
E = 32
TOPK = 8
SEQ_LEN = 1024
SEQS = 32
TOKENS = 32768
BLK = 128
CAPB = 48
KVD = 512
N_SHARD = 16


def touch_ends(values, stream_key, least, largest):
    index_at = [jax.random.randint(jax.random.fold_in(stream_key, axis), (), 0, length) for axis, length in enumerate(values.shape)]
    main_axis = values.shape.index(max(values.shape))
    beside = index_at[:main_axis] + [(index_at[main_axis] + 1) % values.shape[main_axis]] + index_at[main_axis + 1:]
    return values.at[tuple(index_at)].set(least).at[tuple(beside)].set(largest)


def shard_levels(stream_key, shape, split, least, high):
    loudness = 1.0
    for position, blocks in split:
        heights = jax.random.uniform(jax.random.fold_in(jax.random.fold_in(stream_key, 6), position), (blocks,), jnp.float32, least / len(split), high / len(split))
        loudness = loudness * jnp.repeat(jnp.exp(heights), shape[position] // blocks).reshape((-1,) + (1,) * (len(shape) - 1 - position))
    return loudness


def assign_block(stream_key, own, number, rows, count, top, most, slope):
    sequence = jax.random.permutation(stream_key, count)
    packed, usual = load_shares(count, rows * top, most, slope, True), load_shares(count, rows * top, most, slope, False)
    places = jnp.arange(count)

    def named(tallies, rotation):
        used = int((tallies > 0).sum())
        fixed = max(1, used // 4)
        passed = fixed + (places - fixed + rotation * (used - fixed)) % max(1, count - fixed)
        return jnp.zeros((count,), jnp.int32).at[sequence[jnp.where(places < fixed, places, passed)]].set(jnp.asarray(tallies, jnp.int32))

    tallies = jnp.where(number % 4 == 0, named(packed, number // 4), named(usual, number - number // 4 - 1))
    mixed = jax.random.permutation(jax.random.fold_in(own, 3), count)
    giver, taker = mixed[0:count // 2 * 2:2], mixed[1:count // 2 * 2:2]
    slack = jnp.minimum(tallies[giver] - 1, most - tallies[taker]) // 2
    slack = jnp.where((giver == sequence[0]) | (taker == sequence[0]) | (tallies[taker] == 0), 0, jnp.maximum(slack, 0))
    passed = jax.random.randint(jax.random.fold_in(own, 4), (count // 2,), 0, 1 << 20) % (slack + 1)
    tallies = tallies.at[giver].add(-passed).at[taker].add(passed)
    members = jnp.searchsorted(jnp.cumsum(tallies), jnp.arange(rows * top), side="right").astype(jnp.int32)
    listing = members.reshape(top, rows).T
    listing = listing[jax.random.permutation(jax.random.fold_in(own, 1), rows)]
    rotation = jax.random.randint(jax.random.fold_in(own, 2), (rows, 1), 0, top)
    return jnp.take_along_axis(listing, (jnp.arange(top)[None, :] + rotation) % top, axis=1)


def load_shares(amount, total, reach, lean, full):
    weights = [(1 << 20) // math.isqrt(standing ** lean) + 1 for standing in range(1, amount + 1)]
    largest = reach if full else min(reach, max(-(-total // amount), total * weights[0] // sum(weights)))
    least = 1 if total - largest >= amount - 1 else 0
    counts, spare = [largest] + [least] * (amount - 1), total - largest - least * (amount - 1)
    while spare > 0:
        candidates = [i for i in range(1, amount) if counts[i] < largest] or [i for i in range(1, amount) if counts[i] < reach]
        pool, budget = sum([weights[i] for i in candidates]), spare
        for i in candidates:
            extra = min(reach - counts[i], max(1, budget * weights[i] // pool), spare)
            counts[i] = counts[i] + extra
            spare = spare - extra
    return np.array(counts)


def gaussian(stream_key, shape, scale, bound, split=(), kind=jnp.bfloat16):
    level = shard_levels(stream_key, shape, split, -0.22, 0.18) if split else 1.0
    values = jax.random.normal(stream_key, shape, jnp.float32) * scale * level
    return jnp.minimum(jnp.maximum(values, -bound), bound).astype(kind)


def setup_inputs(seed: int = 0) -> dict:
    splits = jax.random.split(jax.random.key(seed), 15)
    hidden_in = gaussian(splits[0], (SEQS, SEQ_LEN, D), 1.0, 6.0, ((0, 16), (1, 8)))
    routes_keys = jax.random.split(jax.random.fold_in(splits[1], 1), SEQS * SEQ_LEN // BLK)
    routes_turns = jax.random.permutation(jax.random.fold_in(splits[1], 3), SEQS * SEQ_LEN // BLK)
    routes = jax.vmap(lambda own, number: assign_block(jax.random.fold_in(splits[1], 2), own, number, BLK, E, TOPK, CAPB, 1))(routes_keys, routes_turns).reshape((SEQS, SEQ_LEN, TOPK))
    prefix = touch_ends(jax.random.randint(splits[2], (SEQS,), SEQ_LEN // 10, SEQ_LEN // 2 + 1), jax.random.fold_in(splits[2], 1), SEQ_LEN // 10, (SEQ_LEN // 2 + 1) - 1).astype(jnp.int32)
    gain_attention = jnp.clip(1.0 + 0.1 * jax.random.normal(splits[3], (D,), jnp.float32), 0.5, 1.5).astype(jnp.bfloat16)
    w_query = gaussian(splits[4], (D, D), D ** -0.5, 0.1875, ((0, 16),))
    w_keyval = gaussian(splits[5], (D, 2 * KVD), D ** -0.5, 0.1875, ((0, 16),))
    gain_query = jnp.clip(1.0 + 0.1 * jax.random.normal(splits[6], (D,), jnp.float32), 0.5, 1.5).astype(jnp.bfloat16)
    gain_key = jnp.clip(1.0 + 0.1 * jax.random.normal(splits[7], (KVD,), jnp.float32), 0.5, 1.5).astype(jnp.bfloat16)
    w_output = gaussian(splits[8], (D, D), (max(D // 256, 1)) ** -0.5, 3.0, ((0, 16),))
    gain_experts = jnp.clip(1.0 + 0.1 * jax.random.normal(splits[9], (D,), jnp.float32), 0.5, 1.5).astype(jnp.bfloat16)
    w_router = gaussian(splits[10], (D, E), (4 * D) ** -0.5, 0.09375, ((0, 16),))
    w_gate_up = gaussian(splits[11], (E, D, 2 * FF), D ** -0.5, 0.1875, ((0, 16), (1, 8)))
    w_down = gaussian(splits[12], (E, FF, D), (FF // 16) ** -0.5, 1.0, ((0, 16), (2, 8)))
    cotangent = gaussian(splits[13], (SEQS, SEQ_LEN, D), 1.0, 6.0, ((0, 16), (1, 8)))
    return dict(hidden_in=hidden_in, routes=routes, prefix=prefix, gain_attention=gain_attention, w_query=w_query, w_keyval=w_keyval, gain_query=gain_query, gain_key=gain_key, w_output=w_output, gain_experts=gain_experts, w_router=w_router, w_gate_up=w_gate_up, w_down=w_down, cotangent=cotangent)


EPSILON = 1e-06
ROPE_BASE = 10000.0
MASKED = -1e+30
EXACT_MODE = lax.Precision.HIGHEST

@jax.custom_vjp
def low(v):
    return lax.optimization_barrier(v.astype(jnp.bfloat16)).astype(jnp.float32)

@jax.custom_vjp
def narrow_backward(v):
    return v

def low_keep(v):
    return (low(v), None)

def low_pass(kept, grad):
    return (grad,)

def back_keep(v):
    return (v, None)

def back_low(kept, grad):
    return (low(grad),)
low.defvjp(low_keep, low_pass)
narrow_backward.defvjp(back_keep, back_low)

def norm_rows(content_vectors_entering, gain_vec):
    return content_vectors_entering * lax.rsqrt(lax.optimization_barrier(jnp.mean(content_vectors_entering * content_vectors_entering, axis=-1, keepdims=True)) + EPSILON) * gain_vec

def rope_tables(positions):
    half_dim = HD // 2
    frequency = ROPE_BASE ** (-2.0 * jnp.arange(half_dim, dtype=jnp.float32) / HD)
    angles = positions.astype(jnp.float32)[:, None] * frequency[None, :]
    return (jnp.cos(angles), jnp.sin(angles))

def apply_spin_phase(heads_in, cosine, sine_table):
    half_dim = HD // 2
    lower_half = heads_in[..., :half_dim]
    upper_half = heads_in[..., half_dim:]
    cos_part = cosine[:, None, :]
    sin_part = sine_table[:, None, :]
    return jnp.concatenate([lower_half * cos_part - upper_half * sin_part, upper_half * cos_part + lower_half * sin_part], axis=-1)

def slot_tables(route_rows, block_len, capacity):
    blocks = route_rows.reshape(-1, block_len * TOPK)
    block_count = blocks.shape[0]
    onehot = (blocks[:, :, None] == jnp.arange(E, dtype=jnp.int32)).astype(jnp.int32)
    slot_index = lax.optimization_barrier(jnp.sum((jnp.cumsum(onehot, axis=1) - 1) * onehot, axis=2))
    block_base = jnp.arange(block_count, dtype=jnp.int32)[:, None] * capacity
    entry_slot = (blocks * (block_count * capacity) + block_base + slot_index).reshape(-1)
    entry_count = entry_slot.shape[0]
    entries = jnp.arange(entry_count, dtype=jnp.int32)
    slot_table = jnp.full((E * block_count * capacity,), entry_count, jnp.int32).at[entry_slot].set(entries)
    return (slot_table.reshape(E, block_count * capacity), entry_slot)

def group_slots(route_group):
    return slot_tables(route_group, BLK, CAPB)[0]

def mixture(expert_rows, gate_rows, slot_table, gate_up_weights, expert_shrink_factors):
    row_count = expert_rows.shape[0]
    tokens_of = slot_table // TOPK
    padded_rows = jnp.concatenate([expert_rows, jnp.zeros((1, D), expert_rows.dtype)])
    padded_gates = jnp.concatenate([gate_rows.reshape(-1), jnp.zeros((1,), gate_rows.dtype)])
    gathered = narrow_backward(padded_rows[tokens_of])
    gate_up = narrow_backward(jnp.einsum('erd,edf->erf', gathered, gate_up_weights, precision=EXACT_MODE))
    middle = low(jax.nn.silu(gate_up[..., :FF]) * gate_up[..., FF:])
    result = narrow_backward(low(jnp.einsum('erf,efd->erd', middle, expert_shrink_factors, precision=EXACT_MODE)))
    weighted = (padded_gates[slot_table][..., None] * result).reshape(-1, D)
    summed = jnp.zeros((row_count + 1, D), result.dtype).at[tokens_of.reshape(-1)].add(weighted)
    return summed[:row_count]

def reference(hidden_in, routes, prefix, gain_attention, w_query, w_keyval, gain_query, gain_key, w_output, gain_experts, w_router, w_gate_up, w_down, cotangent):
    tables = lax.map(group_slots, routes.reshape(N_SHARD, -1, TOPK))
    route_rows = routes.reshape(TOKENS, TOPK)
    positions = jnp.arange(SEQ_LEN, dtype=jnp.int32)
    cosine, sine_table = rope_tables(positions)

    def forward(layer_inputs, gain_one, query_matrix, keyval_matrix, query_gain, key_gain, output_matrix, gain_two, router_weight, gate_up_weights, expert_shrink_factors):
        normalized_rows = low(norm_rows(layer_inputs, gain_one))
        query_rows = narrow_backward(jnp.einsum('owv,vz->owz', normalized_rows, query_matrix, precision=EXACT_MODE))
        keyval_rows = narrow_backward(jnp.einsum('owv,vz->owz', normalized_rows, keyval_matrix, precision=EXACT_MODE))
        keys_raw = keyval_rows[..., :KVD]
        values_low = low(keyval_rows[..., KVD:])
        query_rot = low(apply_spin_phase(norm_rows(query_rows, query_gain).reshape(SEQS, SEQ_LEN, H, HD), cosine, sine_table))
        key_rot = low(apply_spin_phase(norm_rows(keys_raw, key_gain).reshape(SEQS, SEQ_LEN, KVH, HD), cosine, sine_table))
        value_heads = values_low.reshape(SEQS, SEQ_LEN, KVH, HD)

        def attend(pieces):
            query_seq, key_seq, value_seq, prefix_len = pieces
            query_groups = query_seq.reshape(SEQ_LEN, KVH, H // KVH, HD)
            scores = narrow_backward(jnp.einsum('qkgd,lkd->kgql', query_groups, key_seq, precision=EXACT_MODE) * HD ** (-0.5))
            visible = (positions[None, :] <= positions[:, None]) | (positions[None, :] < prefix_len)
            scores = jnp.where(visible, scores, MASKED)
            weights = low(jax.nn.softmax(scores, axis=-1))
            return jnp.einsum('kgql,lkd->qkgd', weights, value_seq, precision=EXACT_MODE).reshape(SEQ_LEN, D)
        attention_result = lax.map(jax.checkpoint(attend), (query_rot, key_rot, value_heads, prefix))
        attention_result = narrow_backward(low(attention_result))
        residual_stream = layer_inputs + narrow_backward(jnp.einsum('owv,vz->owz', attention_result, output_matrix, precision=EXACT_MODE))
        expert_in = low(norm_rows(residual_stream, gain_two)).reshape(TOKENS, D)
        logits = narrow_backward(jnp.dot(expert_in, router_weight, precision=EXACT_MODE))
        gate_probs = jax.nn.softmax(jnp.take_along_axis(logits, route_rows, axis=1), axis=-1)

        def run_group(pieces):
            return mixture(pieces[0], pieces[1], pieces[2], gate_up_weights, expert_shrink_factors)
        moe_out = lax.map(jax.checkpoint(run_group), (expert_in.reshape(N_SHARD, -1, D), gate_probs.reshape(N_SHARD, -1, TOPK), tables))
        return residual_stream + moe_out.reshape(SEQS, SEQ_LEN, D)
    floats = tuple((array.astype(jnp.float32) for array in (hidden_in, gain_attention, w_query, w_keyval, gain_query, gain_key, w_output, gain_experts, w_router, w_gate_up, w_down)))
    primal, pullback = jax.vjp(forward, *floats)
    gradients = pullback(cotangent.astype(jnp.float32))
    return (primal.astype(jnp.bfloat16), gradients[0].astype(jnp.bfloat16), gradients[1], gradients[2], gradients[3], gradients[4], gradients[5], gradients[6], gradients[7], gradients[8], gradients[9], gradients[10])
```

```python
import functools

import jax
import jax.numpy as jnp
from jax import lax
from jax.experimental import pallas as pl
from jax.experimental.pallas import tpu as pltpu
from jax.sharding import PartitionSpec as P

D = 1024
KVH = 8
HD = 64
FF = 512
E = 32
SEQ_LEN = 1024
BLK = 128
SEQS = 2
ROWS = SEQS * BLK
CAP = 48
SLOTS = 4 * CAP
N_SHARD = 16
N_CTX = 8
PAIRS = 8
LANE = 128
QB = 256
EPSILON = 1e-06
ROPE_BASE = 10000.0
MASKED = -1e30
F32 = jnp.float32
BF16 = jnp.bfloat16

LANES = [[c + 2 * k for k in range(PAIRS)] for c in range(2)]
CHIPS = [[(c + 2 * k) * N_CTX + j for k in range(PAIRS) for j in range(N_CTX)] for c in range(2)]
OTHER_CORE = [(i, i ^ 1) for i in range(N_SHARD)]
X_HI = [(i, i ^ 4) for i in range(N_CTX)]
FIRST = 2 * D + 2 * LANE
LAST = 2 * D + LANE


def y_shift(step):
    return [(i, i // 4 * 4 + (i + step) % 4) for i in range(N_CTX)]


def dot(a, b):
    return jnp.dot(a, b, preferred_element_type=F32)


def dot_nt(a, b):
    return lax.dot_general(a, b, (((1,), (1,)), ((), ())), preferred_element_type=F32)


def dot_tn(a, b):
    return lax.dot_general(a, b, (((0,), (0,)), ((), ())), preferred_element_type=F32)


def lane_of(shape):
    return lax.broadcasted_iota(jnp.int32, shape, len(shape) - 1)


def inverse_scale(z):
    return lax.rsqrt(jnp.mean(z * z, axis=-1, keepdims=True) + EPSILON)


def swap_halves(x):
    first = lane_of(x.shape) % HD < HD // 2
    return jnp.where(first, pltpu.roll(x, LANE - HD // 2, 1), pltpu.roll(x, HD // 2, 1))


def side(h):
    return slice(h * LANE, (h + 1) * LANE)


def kernel_call(body, out, flops=0, nbytes=0, mb=48, **kwargs):
    return pl.pallas_call(
        body,
        out_shape=out,
        compiler_params=pltpu.CompilerParams(vmem_limit_bytes=mb * 2**20),
        cost_estimate=pl.CostEstimate(flops=flops, bytes_accessed=nbytes, transcendentals=0),
        **kwargs,
    )


def struct(shape, dtype):
    return jax.ShapeDtypeStruct(shape, dtype)


def key_lanes(shape):
    return lane_of(shape) % LANE < HD


def kv_scale(kv_raw):
    keys = key_lanes(kv_raw.shape)
    total = jnp.sum(jnp.where(keys, kv_raw * kv_raw, 0.0), axis=-1, keepdims=True)
    return lax.rsqrt(total / (D // 2) + EPSILON), keys


def turned_gains(block):
    rows = block.astype(F32).T[0:8]
    place = lane_of(rows.shape) % LANE
    keys = jnp.where(place < HD // 2, rows, pltpu.roll(rows, D - HD // 2, 1))
    keys = jnp.where(place < HD, keys, 1.0)
    which = lax.broadcasted_iota(jnp.int32, rows.shape, 0)
    return jnp.where(which == 2, keys, rows)


def front_body(x_ref, w_ref, rope_ref, packed_ref, normed_ref, q_ref, kv_ref, gains_ref):
    x = x_ref[...].astype(F32)
    gains = turned_gains(w_ref[:, LAST:FIRST])
    gains_ref[...] = gains
    normed = (x * inverse_scale(x) * gains[0:1]).astype(BF16)
    normed_ref[...] = normed
    q = dot(normed, w_ref[:, 0:D])
    kv = dot(normed, w_ref[:, D : 2 * D])
    q_ref[...] = q
    kv_ref[...] = kv
    r_k, keys = kv_scale(kv)
    qn = q * inverse_scale(q) * gains[1:2]
    kn = kv * jnp.where(keys, r_k * gains[2:3], 1.0)
    c, s, ck, sk = rope_ref[0], rope_ref[1], rope_ref[2], rope_ref[3]
    for h in range(KVH):
        qh, kh = qn[:, side(h)], kn[:, side(h)]
        packed_ref[h, :, 0:LANE] = (qh * c + swap_halves(qh) * s).astype(BF16)
        packed_ref[h, :, LANE : 2 * LANE] = (kh * ck + swap_halves(kh) * sk).astype(BF16)


def front(x, first, rope):
    return kernel_call(
        front_body,
        (
            struct((KVH, ROWS, 2 * LANE), BF16),
            struct((ROWS, D), BF16),
            struct((ROWS, D), F32),
            struct((ROWS, D), F32),
            struct((8, D), F32),
        ),
        flops=2 * ROWS * D * 2 * D,
        nbytes=9 * 2**20,
    )(x, first, rope)


def key_extent(qb):
    return max((qb + 1) * QB, SEQ_LEN // 2)


def both_halves(kv):
    kv = kv.astype(F32)
    turned = pltpu.roll(kv, HD, 1)
    low = lane_of(kv.shape) < HD
    return jnp.where(low, kv, turned).astype(BF16), jnp.where(low, turned, kv).astype(BF16)


def attend_body(prefix_ref, in_ref, out_ref):
    length = prefix_ref[pl.program_id(0)]
    rows = in_ref[...].reshape(SEQ_LEN, 2 * LANE)
    q = rows[:, :LANE] * jnp.asarray(HD**-0.5, BF16)
    k2, v2 = both_halves(rows[:, LANE:])
    group = lane_of((SEQ_LEN, LANE)) // HD
    zero = jnp.zeros((), BF16)
    values = [jnp.where(group == g, v2, zero) for g in range(2)]
    for qb in range(SEQ_LEN // QB):
        lo, hi = qb * QB, key_extent(qb)
        i = lo + lax.broadcasted_iota(jnp.int32, (QB, hi - lo), 0)
        j = lo + lane_of((QB, hi - lo))
        seen = (j <= i) | (j < length)
        total = jnp.zeros((QB, LANE), F32)
        for g in range(2):
            qg = jnp.where(group[lo : lo + QB] == g, q[lo : lo + QB], zero)
            near = jnp.where(seen, dot_nt(qg, k2[lo:hi]), MASKED)
            peak = jnp.max(near, axis=1, keepdims=True)
            if lo:
                far = dot_nt(qg, k2[:lo])
                peak = jnp.maximum(peak, jnp.max(far, axis=1, keepdims=True))
            near = jnp.exp(near - peak)
            norm = jnp.sum(near, axis=1, keepdims=True)
            out = dot(near.astype(BF16), values[g][lo:hi])
            if lo:
                far = jnp.exp(far - peak)
                norm = norm + jnp.sum(far, axis=1, keepdims=True)
                out = out + dot(far.astype(BF16), values[g][:lo])
            total = total + out / norm
        out_ref[2 * qb : 2 * qb + 2] = total.astype(BF16).reshape(2, BLK, LANE)


def attend(prefix, rows):
    return kernel_call(
        attend_body,
        struct((N_CTX, ROWS, LANE), BF16),
        flops=2 * 2 * 2 * 1024 * 1024 * 128,
        nbytes=2 * 2**20,
        grid=(SEQS,),
        in_specs=[
            pl.BlockSpec(memory_space=pltpu.SMEM),
            pl.BlockSpec((N_CTX, BLK, 2 * LANE), lambda s: (0, s, 0)),
        ],
        out_specs=pl.BlockSpec((N_CTX, BLK, LANE), lambda s: (0, s, 0)),
    )(prefix, rows)


def attend_back_body(prefix_ref, in_ref, grad_ref, out_ref, dk_ref, dv_ref):
    length = prefix_ref[pl.program_id(0)]
    rows = in_ref[...].reshape(SEQ_LEN, 2 * LANE)
    q = rows[:, :LANE] * jnp.asarray(HD**-0.5, BF16)
    k2, v2 = both_halves(rows[:, LANE:])
    grad = grad_ref[...].reshape(SEQ_LEN, LANE)
    group = lane_of((SEQ_LEN, LANE)) // HD
    zero = jnp.zeros((), BF16)
    keys = [jnp.where(group == g, k2, zero) for g in range(2)]
    dk_ref[...] = jnp.zeros_like(dk_ref)
    dv_ref[...] = jnp.zeros_like(dv_ref)
    for qb in range(SEQ_LEN // QB):
        lo, hi = qb * QB, key_extent(qb)
        i = lo + lane_of((hi - lo, QB))
        j = lo + lax.broadcasted_iota(jnp.int32, (hi - lo, QB), 0)
        seen = (j <= i) | (j < length)
        dq = jnp.zeros((QB, LANE), F32)
        for g in range(2):
            mine = group[lo : lo + QB] == g
            qg = jnp.where(mine, q[lo : lo + QB], zero)
            gg = jnp.where(mine, grad[lo : lo + QB], zero)
            spans = [(lo, hi)] + ([(0, lo)] if lo else [])
            scores = [dot_nt(k2[a:b], qg) for a, b in spans]
            scores[0] = jnp.where(seen, scores[0], MASKED)
            peak = functools.reduce(jnp.maximum, [jnp.max(s, axis=0, keepdims=True) for s in scores])
            scores = [jnp.exp(s - peak) for s in scores]
            norm = 1.0 / sum(jnp.sum(s, axis=0, keepdims=True) for s in scores)
            scores = [s * norm for s in scores]
            grads = [dot_nt(v2[a:b], gg) for a, b in spans]
            inner = sum(jnp.sum(s * d, axis=0, keepdims=True) for s, d in zip(scores, grads))
            for (a, b), s, d in zip(spans, scores, grads):
                ds = (s * (d - inner)).astype(BF16)
                dv_ref[a:b] += dot(s.astype(BF16), gg)
                dk_ref[a:b] += dot(ds, qg)
                dq = dq + dot_tn(ds, keys[g][a:b])
        out_ref[2 * qb : 2 * qb + 2, :, 0:LANE] = (dq * HD**-0.5).astype(BF16).reshape(2, BLK, LANE)
    dk = dk_ref[...]
    dv = dv_ref[...]
    dk = dk + pltpu.roll(dk, HD, 1)
    dv = dv + pltpu.roll(dv, HD, 1)
    out = jnp.where(lane_of(dk.shape) < HD, dk, dv).astype(BF16)
    out_ref[:, :, LANE : 2 * LANE] = out.reshape(N_CTX, BLK, LANE)


def attend_back(prefix, rows, grad):
    return kernel_call(
        attend_back_body,
        struct((N_CTX, ROWS, 2 * LANE), BF16),
        flops=2 * 5 * 2 * 1024 * 1024 * 128,
        nbytes=3 * 2**20,
        grid=(SEQS,),
        in_specs=[
            pl.BlockSpec(memory_space=pltpu.SMEM),
            pl.BlockSpec((N_CTX, BLK, 2 * LANE), lambda s: (0, s, 0)),
            pl.BlockSpec((N_CTX, BLK, LANE), lambda s: (0, s, 0)),
        ],
        out_specs=pl.BlockSpec((N_CTX, BLK, 2 * LANE), lambda s: (0, s, 0)),
        scratch_shapes=[pltpu.VMEM((SEQ_LEN, LANE), F32), pltpu.VMEM((SEQ_LEN, LANE), F32)],
    )(prefix, rows, grad)


def middle_body(x_ref, att_ref, wo_ref, gains_ref, residual_ref, attended_ref, in_ref, copy_ref):
    for h in range(KVH):
        attended_ref[:, side(h)] = att_ref[h]
    wo = wo_ref[:, :, 0:D].reshape(D, D)
    copy_ref[...] = wo
    residual = x_ref[...].astype(F32) + dot(attended_ref[...], wo)
    residual_ref[...] = residual
    in_ref[...] = (residual * inverse_scale(residual) * gains_ref[3:4]).astype(BF16)


def middle(x, att, all_out, gains):
    full = lambda *shape: pl.BlockSpec(shape, lambda i: (0,) * len(shape))
    return kernel_call(
        middle_body,
        (struct((ROWS, D), F32), struct((ROWS, D), BF16), struct((ROWS, D), BF16), struct((D, D), BF16)),
        flops=2 * ROWS * D * D,
        nbytes=7 * 2**20,
        grid=(1,),
        in_specs=[
            full(ROWS, D),
            full(KVH, ROWS, LANE),
            pl.BlockSpec((N_SHARD, 64, D + LANE), lambda i: (0, ROWS // 64, 0)),
            full(8, D),
        ],
        out_specs=(full(ROWS, D),) * 3 + (full(D, D),),
    )(x, att, all_out, gains)


def softmax_over(logits, member):
    logits = jnp.where(member, logits, MASKED)
    e = jnp.exp(logits - jnp.max(logits, axis=-1, keepdims=True))
    return e / jnp.sum(e, axis=-1, keepdims=True)


def split_two(v):
    high = v.astype(BF16)
    return high, (v - high.astype(F32)).astype(BF16)


def experts_body(
    me_ref, x_ref, g_ref, slot_ref, router_ref, p0, p1, p2, p3, p4, p5, p6, p7,
    back_keep, back_give, out_ref, gg_ref, xr_ref, go_ref, mid_ref, dgu_ref,
    wo_ref, gd_ref, gr_ref, w_ref, sem,
):
    shard = me_ref[0]

    @pl.when(pl.program_id(0) == 0)
    def _():
        copies = []
        for n, piece in enumerate((p0, p1, p2, p3, p4, p5, p6, p7)):
            at = pl.multiple_of(me_ref[1 + n] * BLK, BLK)
            for e in range(2):
                copies.append(
                    pltpu.make_async_copy(piece.at[e], w_ref.at[e, pl.ds(at, BLK)], sem.at[2 * n + e])
                )
        for copy in copies:
            copy.start()
        for copy in copies:
            copy.wait()

    core = lax.rem(shard, 2)
    sources = [(k, j, lax.rem(core + j, 2)) for k in range(2) for j in range(2)]
    picks = []
    for n, (k, j, c) in enumerate(sources):
        slots = slot_ref[k, c]
        want = lax.broadcasted_iota(jnp.int32, (2 * CAP, ROWS), 0).astype(F32)
        pick = jnp.concatenate(
            [(slots[e : e + 1] == want).astype(F32) for e in range(2)], axis=0
        ).astype(BF16)
        picks.append(pick)
        x = x_ref[k, c]
        grads = g_ref[k, c, :, 0:D]
        member = g_ref[k, c, :, D : D + LANE].astype(F32) > 0
        gates = softmax_over(dot(x, router_ref[...]), member)
        high, low = split_two(gates)
        at = dot(pick, high) + dot(pick, low)
        lane = lane_of(at.shape) - shard * 8
        expert = lax.broadcasted_iota(jnp.int32, at.shape, 0) // (2 * CAP)
        gate = jnp.sum(jnp.where(lane == expert, at, 0.0), axis=-1, keepdims=True)
        rows = dot(pick, x).astype(BF16)
        grad_rows = dot(pick, grads)
        scaled = (gate * grad_rows).astype(BF16)
        grad_rows = grad_rows.astype(BF16)
        place = slice(n * 2 * CAP, (n + 1) * 2 * CAP)
        for e in range(2):
            part = slice(e * 2 * CAP, (e + 1) * 2 * CAP)
            xr_ref[e, place] = rows[part]
            go_ref[e, place] = scaled[part]
            gr_ref[e, place] = grad_rows[part]
            gd_ref[e, place] = jnp.broadcast_to(gate[part], (2 * CAP, LANE))
    dots = []
    for e in range(2):
        gate_up = dot(xr_ref[e], w_ref[e, :, 0 : 2 * FF])
        g, u = gate_up[:, :FF], gate_up[:, FF:]
        sig = 1.0 / (1.0 + jnp.exp(-g))
        act = g * sig
        mid = (act * u).astype(BF16)
        mid_ref[e] = mid
        out = dot_nt(mid, w_ref[e, :, 2 * FF :]).astype(BF16).astype(F32)
        dots.append(jnp.sum(out * gr_ref[e].astype(F32), axis=-1, keepdims=True))
        wo_ref[e] = (out * gd_ref[e, :, 0:1]).astype(BF16)
        grad_mid = dot(go_ref[e], w_ref[e, :, 2 * FF :])
        dgu_ref[e, :, 0:FF] = (grad_mid * u * sig * (1.0 + g * (1.0 - sig))).astype(BF16)
        dgu_ref[e, :, FF : 2 * FF] = (grad_mid * act).astype(BF16)
        gr_ref[e] = dot_nt(dgu_ref[e], w_ref[e, :, 0 : 2 * FF]).astype(BF16)
    for n, (k, j, c) in enumerate(sources):
        place = slice(n * 2 * CAP, (n + 1) * 2 * CAP)
        pick = picks[n]
        back = dot_tn(pick, jnp.concatenate([gr_ref[0, place], gr_ref[1, place]], axis=0))
        out = dot_tn(pick, jnp.concatenate([wo_ref[0, place], wo_ref[1, place]], axis=0))
        (back_give if j else back_keep)[k] = back.astype(BF16)
        out_ref[k, c] = out.astype(BF16)
        values = jnp.concatenate([dots[0][place], dots[1][place]], axis=0)
        lane = lane_of((SLOTS, LANE))
        expert = lax.broadcasted_iota(jnp.int32, (SLOTS, LANE), 0) // (2 * CAP)
        high, low = split_two(jnp.where(lane == expert, values, 0.0))
        gg_ref[k, c] = (dot_tn(high, pick) + dot_tn(low, pick))[0:8]


def experts(places, x, grads, slots, router, pieces):
    steps = 4
    per = 2 * 4 * CAP
    half = pl.BlockSpec((2, ROWS, D), lambda i: (i, 0, 0))
    kept = lambda width: pl.BlockSpec((2, per, width), lambda i: (0, i, 0))
    whole = lambda shape: pl.BlockSpec(shape, lambda i: (0,) * len(shape), pipeline_mode=pl.Buffered(1))
    total = steps * per
    return kernel_call(
        experts_body,
        (struct((PAIRS, ROWS, D), BF16),) * 2
        + (
            struct((PAIRS, 2, ROWS, D), BF16),
            struct((PAIRS, 2, 8, ROWS), F32),
            struct((2, total, D), BF16),
            struct((2, total, D), BF16),
            struct((2, total, FF), BF16),
            struct((2, total, 2 * FF), BF16),
        ),
        flops=30 * 10**9,
        nbytes=60 * 2**20,
        mb=60,
        grid=(steps,),
        in_specs=[
            pl.BlockSpec(memory_space=pltpu.SMEM),
            pl.BlockSpec((2, 2, ROWS, D), lambda i: (i, 0, 0, 0)),
            pl.BlockSpec((2, 2, ROWS, D + LANE), lambda i: (i, 0, 0, 0)),
            pl.BlockSpec((2, 2, 2, ROWS), lambda i: (i, 0, 0, 0)),
            whole((D, LANE)),
        ]
        + [pl.BlockSpec(memory_space=pl.ANY)] * 8,
        out_specs=(half,) * 2
        + (
            pl.BlockSpec((2, 2, ROWS, D), lambda i: (i, 0, 0, 0)),
            pl.BlockSpec((2, 2, 8, ROWS), lambda i: (i, 0, 0, 0)),
            kept(D), kept(D), kept(FF), kept(2 * FF),
        ),
        scratch_shapes=[
            pltpu.VMEM((2, per, D), BF16),
            pltpu.VMEM((2, per, LANE), F32),
            pltpu.VMEM((2, per, D), BF16),
            pltpu.VMEM((2, D, 3 * FF), BF16),
            pltpu.SemaphoreType.DMA((16,)),
        ],
    )(places, x, grads, slots, router, *pieces)


def expert_grads_body(me_ref, xa_ref, xb_ref, ga_ref, gb_ref, mid_ref, dgu_ref, *out_refs):
    values = []
    for e in range(2):
        rows = jnp.concatenate([xa_ref[e], xb_ref[e]], axis=1)
        values.append(dot_tn(rows, dgu_ref[e]).astype(BF16))
        rows = jnp.concatenate([ga_ref[e], gb_ref[e]], axis=1)
        values.append(dot_tn(rows, mid_ref[e]).astype(BF16))
    for step, out_ref in enumerate(out_refs):

        @pl.when(pl.program_id(0) == step)
        def _():
            for e in range(2):
                for half in range(2):
                    part = slice(half * BLK, (half + 1) * BLK)
                    out_ref[half, e, :, 0 : 2 * FF] = values[2 * e][part]
                    out_ref[half, e, :, 2 * FF :] = values[2 * e + 1][part]


def expert_grads(places, rows_in, rows_grad, mid, dgu):
    total = rows_in.shape[1]
    column = lambda half: pl.BlockSpec((2, total, BLK), lambda t, me: (0, 0, me[1 + 2 * t + half]))
    whole = lambda width: pl.BlockSpec((2, total, width), lambda t, me: (0, 0, 0))
    piece = (2, 2, BLK, 3 * FF)
    return kernel_call(
        expert_grads_body,
        (struct(piece, BF16),) * 4,
        flops=2 * 2 * total * D * 3 * FF,
        nbytes=30 * 2**20,
        grid_spec=pltpu.PrefetchScalarGridSpec(
            num_scalar_prefetch=1,
            grid=(4,),
            in_specs=[column(0), column(1), column(0), column(1), whole(FF), whole(2 * FF)],
            out_specs=(pl.BlockSpec(piece, lambda t, me: (0, 0, 0, 0)),) * 4,
        ),
    )(places, rows_in, rows_in, rows_grad, rows_grad, mid, dgu)


def norm_back(z, r, gain, grad):
    weighted = grad * gain
    inner = jnp.mean(weighted * z, axis=-1, keepdims=True)
    return r * weighted - z * (r * r * r) * inner, jnp.sum(grad * z * r, axis=0, keepdims=True)


def turn_body(
    parts_ref, gg_ref, in_ref, residual_ref, cot_ref, routes_ref, router_ref, gains_ref, wo_ref,
    gatt_ref, gres_ref, gattn_ref, glog_ref, ggain_ref,
):
    member = routes_ref[...].astype(F32) > 0
    gates = softmax_over(dot(in_ref[...], router_ref[...]), member)
    gg = gg_ref[...].reshape(LANE, ROWS).T
    chosen = gates * (gg - jnp.sum(gates * gg, axis=-1, keepdims=True))
    glog = chosen.astype(BF16)
    glog_ref[...] = glog
    grad = dot_nt(glog, router_ref[...])
    for n in range(PAIRS):
        grad = grad + parts_ref[n].astype(F32)
    residual = residual_ref[...]
    gz, ggain = norm_back(residual, inverse_scale(residual), gains_ref[3:4], grad)
    ggain_ref[...] = ggain
    gres = cot_ref[...].astype(F32) + gz
    gres_ref[...] = gres
    gattn = gres.astype(BF16)
    gattn_ref[...] = gattn
    gatt = dot_nt(gattn, wo_ref[...]).astype(BF16)
    for h in range(KVH):
        gatt_ref[h] = gatt[:, side(h)]


def turn(parts, gg, expert_in, residual, cot, member, router, gains, wo):
    return kernel_call(
        turn_body,
        (
            struct((KVH, ROWS, LANE), BF16),
            struct((ROWS, D), F32),
            struct((ROWS, D), BF16),
            struct((ROWS, LANE), BF16),
            struct((1, D), F32),
        ),
        flops=2 * ROWS * D * D,
        nbytes=10 * 2**20,
    )(parts, gg, expert_in, residual, cot, member, router, gains, wo)


def finish_body(
    me_ref, rows_ref, q_ref, kv_ref, x_ref, normed_ref, gres_ref, w_ref, gains_ref, rope_ref, side_ref, gaine_ref,
    grad_in_ref, keep_ref, give_ref, gq_ref, gk_ref, gw_ref,
):
    core = lax.rem(me_ref[0], 2)
    gains = gains_ref[...]
    c, s, ck, sk = rope_ref[0], rope_ref[1], rope_ref[2], rope_ref[3]
    for h in range(KVH):
        gh = rows_ref[h, :, 0:LANE].astype(F32)
        kh = rows_ref[h, :, LANE : 2 * LANE].astype(F32)
        gq_ref[:, side(h)] = gh * c - swap_halves(gh) * s
        gk_ref[:, side(h)] = kh * ck - swap_halves(kh) * sk
    q = q_ref[...]
    gq, gain_q = norm_back(q, inverse_scale(q), gains[1:2], gq_ref[...])
    gq = gq.astype(BF16)
    kv, gkv = kv_ref[...], gk_ref[...]
    r, keys = kv_scale(kv)
    weighted = jnp.where(keys, gkv * gains[2:3], 0.0)
    inner = jnp.sum(weighted * kv, axis=-1, keepdims=True) / (D // 2)
    gk = jnp.where(keys, r * weighted - kv * (r * r * r) * inner, gkv).astype(BF16)
    gain_k = jnp.sum(jnp.where(keys, gkv * kv * r, 0.0), axis=0, keepdims=True)
    normed = normed_ref[...]
    gw_ref[:, :, 0:D] = dot_tn(normed, gq).astype(BF16).reshape(N_SHARD, 64, D)
    gw_ref[:, :, D : 2 * D] = dot_tn(normed, gk).astype(BF16).reshape(N_SHARD, 64, D)
    grad = dot_nt(gq, w_ref[:, 0:D]) + dot_nt(gk, w_ref[:, D : 2 * D])
    x = x_ref[...].astype(F32)
    gx, gain_a = norm_back(x, inverse_scale(x), gains[0:1], grad)
    grad_in_ref[...] = (gres_ref[...] + gx).astype(BF16)
    zero = jnp.zeros((2, D), F32)
    rows = jnp.concatenate([zero, gain_a, gain_q, gain_k, gaine_ref[...], zero], axis=0)
    which = lax.broadcasted_iota(jnp.int32, rows.shape, 0)
    place = lane_of(rows.shape) % LANE
    rows = jnp.where((which == 4) & (place >= HD), pltpu.roll(rows, HD // 2, 1), rows)
    rows = jnp.concatenate([rows, jnp.zeros((LANE - 8, D), F32)], axis=0)
    beside = (side_ref[...] + rows.T).astype(BF16)
    gw_ref[:, :, 2 * D : LAST] = beside.reshape(N_SHARD, 64, LANE)
    for k in range(PAIRS):
        keep_ref[k] = gw_ref[2 * k + core]
        give_ref[k] = gw_ref[2 * k + 1 - core]


def finish(places, rows, q, kv, x, normed, gres, first, gains, rope, beside, gain_e):
    vmem = pl.BlockSpec(memory_space=pltpu.VMEM)
    return kernel_call(
        finish_body,
        (struct((ROWS, D), BF16),) + (struct((PAIRS, 64, LAST), BF16),) * 2,
        flops=4 * 2 * ROWS * D * D,
        nbytes=15 * 2**20,
        in_specs=[pl.BlockSpec(memory_space=pltpu.SMEM)] + [vmem] * 11,
        scratch_shapes=[
            pltpu.VMEM((ROWS, D), F32),
            pltpu.VMEM((ROWS, D), F32),
            pltpu.VMEM((N_SHARD, 64, LAST), BF16),
        ],
    )(places, rows, q, kv, x, normed, gres, first, gains, rope, beside, gain_e)


def project_back_body(
    me_ref, att_ref, gattn_ref, in_ref, glog_ref, keep_ref, give_ref, beside_ref, gw_ref
):
    core = lax.rem(me_ref[0], 2)
    gw_ref[...] = dot_tn(att_ref[...], gattn_ref[...]).astype(BF16).reshape(N_SHARD, 64, D)
    for k in range(PAIRS):
        keep_ref[k] = gw_ref[2 * k + core]
        give_ref[k] = gw_ref[2 * k + 1 - core]
    beside_ref[...] = dot_tn(in_ref[...], glog_ref[...])


def project_back(places, attended, gattn, expert_in, glog):
    vmem = pl.BlockSpec(memory_space=pltpu.VMEM)
    return kernel_call(
        project_back_body,
        (struct((PAIRS, 64, D), BF16),) * 2 + (struct((D, LANE), F32),),
        flops=2 * ROWS * D * D,
        nbytes=6 * 2**20,
        in_specs=[pl.BlockSpec(memory_space=pltpu.SMEM)] + [vmem] * 4,
        scratch_shapes=[pltpu.VMEM((N_SHARD, 64, D), BF16)],
    )(places, attended, gattn, expert_in, glog)


def interleave(kv):
    return jnp.swapaxes(kv.reshape(-1, 2, KVH, HD), 1, 2).reshape(-1, D)


def separate(kv):
    return jnp.swapaxes(kv.reshape(-1, KVH, 2, HD), 1, 2).reshape(-1, D)


def spread(per_expert):
    rows = per_expert.shape[0]
    padded = jnp.pad(per_expert.reshape(rows, N_SHARD, 2), ((0, 0), (0, 0), (0, 6)))
    return padded.reshape(rows, LANE)


def rope_tables(ctx):
    half = HD // 2
    positions = ctx * BLK + jnp.arange(BLK, dtype=jnp.int32)
    frequency = ROPE_BASE ** (-2.0 * jnp.arange(half, dtype=F32) / HD)
    angles = positions.astype(F32)[:, None] * frequency[None, :]
    c, s = jnp.cos(angles), jnp.sin(angles)
    c, s = jnp.concatenate([c, c], axis=1), jnp.concatenate([-s, s], axis=1)
    one, zero = jnp.ones_like(c), jnp.zeros_like(c)
    pairs = [(c, c), (s, s), (c, one), (s, zero)]
    tables = jnp.stack([jnp.concatenate(p, axis=1) for p in pairs])
    return jnp.concatenate([tables] * SEQS, axis=1)


def to_every(own, axis):
    count = lax.axis_size(axis)
    copies = jnp.broadcast_to(own[None], (count,) + own.shape)
    return lax.all_to_all(copies, axis, 0, 0, tiled=True)


def with_other_core(keep, give):
    got = lax.ppermute(give, "shard", OTHER_CORE)
    return (keep.astype(F32) + got.astype(F32)).astype(BF16)


def local(
    hidden_in,
    routes,
    prefix,
    gain_attention,
    w_query,
    w_keyval,
    gain_query,
    gain_key,
    w_output,
    gain_experts,
    w_router,
    w_gate_up,
    w_down,
    cotangent,
):
    shard = lax.axis_index("shard")
    ctx = lax.axis_index("ctx")
    core = shard % 2
    x = hidden_in.reshape(ROWS, D)
    cot = cotangent.reshape(ROWS, D)

    key_rows = jnp.pad(gain_key, (0, 32))
    columns = jnp.stack([gain_attention, gain_query, key_rows, gain_experts], axis=1)
    first = lax.all_gather(
        jnp.concatenate(
            [w_query, interleave(w_keyval), spread(w_router), jnp.pad(columns, ((0, 0), (0, LANE - 4)))],
            axis=1,
        ),
        "shard",
        axis=0,
        tiled=True,
    )
    router = first[:, 2 * D : LAST]
    own_w = jnp.concatenate([w_gate_up, jnp.swapaxes(w_down, 1, 2)], axis=2)
    other_w = lax.ppermute(own_w, "ctx", X_HI)
    up, down, far = (lax.ppermute(own_w, "ctx", y_shift(step)) for step in (1, -1, 2))
    x, own_w, other_w, up, down, far = lax.optimization_barrier((x, own_w, other_w, up, down, far))
    high, low = ctx // 4 * 4, ctx % 4
    sources = []
    for step in (0, -1, 1, 2):
        sources += [high + (low + step) % 4, 4 - high + (low + step) % 4]
    places = jnp.stack([shard, *sources]).astype(jnp.int32)

    lanes = jnp.arange(LANE, dtype=jnp.int32)
    named = jnp.where(lanes % 8 < 2, lanes // 8 * 2 + lanes % 8, -1)
    member = jnp.any(routes.reshape(ROWS, -1)[:, :, None] == named, axis=1).astype(BF16)
    sent = jnp.concatenate([cot, member], axis=1)
    sent = jnp.concatenate([sent, jnp.pad(w_output, ((0, 0), (0, LANE)))])
    all_out = lax.all_gather(sent, "shard", axis=0)
    own_member = lax.dynamic_slice(all_out, (0, 0, D + 8 * shard), (N_SHARD, ROWS, 2))
    own_member = own_member.reshape(N_SHARD, SEQS, BLK, 2)
    earlier = jnp.tril(jnp.ones((BLK, BLK), BF16), -1)
    slots = jnp.einsum("ts,nbse->nebt", earlier, own_member, preferred_element_type=F32)
    slots = slots + jnp.arange(SEQS, dtype=F32)[:, None] * CAP
    slots = jnp.where(jnp.transpose(own_member, (0, 3, 1, 2)) > 0, slots, -1.0)
    slots = slots.reshape(PAIRS, 2, 2, ROWS)

    rope = rope_tables(ctx)
    packed, normed, q_raw, kv_raw, gains = front(x, first, rope)
    packed = lax.all_to_all(packed, "ctx", 0, 0, tiled=True)
    att = lax.all_to_all(attend(prefix, packed), "ctx", 0, 0, tiled=True)
    residual, attended, expert_in, wo = middle(x, att, all_out, gains)

    all_in = lax.all_gather(expert_in, "shard", axis=0)
    other, _ = lax.optimization_barrier((other_w, expert_in))
    other_up, other_down, other_far = (lax.ppermute(other, "ctx", y_shift(step)) for step in (1, -1, 2))
    back_keep, back_give, out, gg, rows_in, rows_grad, mid, dgu = experts(
        places,
        all_in.reshape(PAIRS, 2, ROWS, D),
        all_out.reshape(PAIRS, 2, ROWS + 64, D + LANE),
        slots,
        router,
        (own_w, other_w, up, other_up, down, other_down, far, other_far),
    )
    gg = lax.all_to_all(gg.reshape(N_SHARD, 8, ROWS), "shard", 0, 0, tiled=True)
    both = with_other_core(back_keep, back_give)
    both, gg, rows_in = lax.optimization_barrier((both, gg, rows_in))
    parts = lax.all_to_all(both, "shard", 0, 0, tiled=True, axis_index_groups=LANES)
    gw_own, gw_down, gw_up, gw_far = expert_grads(places, rows_in, rows_grad, mid, dgu)
    gw_down = lax.ppermute(gw_down, "ctx", y_shift(-1))
    gw_up = lax.ppermute(gw_up, "ctx", y_shift(1))
    gw_far = lax.ppermute(gw_far, "ctx", y_shift(2))
    parts, gw_up, gw_down = lax.optimization_barrier((parts, gw_up, gw_down))
    gatt, gres, gattn, glog, gain_e = turn(
        parts, gg, expert_in, residual, cot, member, router, gains, wo
    )

    gattn, out = lax.optimization_barrier((gattn, out))

    gatt = lax.all_to_all(gatt, "ctx", 0, 0, tiled=True)
    grads = lax.all_to_all(attend_back(prefix, packed, gatt), "ctx", 0, 0, tiled=True)
    grads, gw_far = lax.optimization_barrier((grads, gw_far))
    wo_keep, wo_give, beside = project_back(places, attended, gattn, expert_in, glog)
    grad_input, gw_keep, gw_give = finish(
        places, grads, q_raw, kv_raw, x, normed, gres, first, gains, rope, beside, gain_e
    )

    moe = lax.psum_scatter(
        out.reshape(N_SHARD, ROWS, D), "shard", scatter_dimension=0, tiled=True
    )
    layer_out = (residual + moe[0].astype(F32)).astype(BF16)

    pieces = sum(g.astype(F32) for g in (gw_own, gw_up, gw_down, gw_far)).astype(BF16)
    pieces = pieces[0].astype(F32) + lax.ppermute(pieces[1], "ctx", X_HI).astype(F32)
    dense = with_other_core(
        jnp.concatenate([gw_keep, wo_keep], axis=2), jnp.concatenate([gw_give, wo_give], axis=2)
    )
    dense = dense.reshape(PAIRS * N_CTX, 8, -1)
    dense = lax.all_to_all(dense, ("shard", "ctx"), 0, 0, tiled=True, axis_index_groups=CHIPS)
    dense = to_every(dense.astype(F32).sum(axis=0).astype(BF16), "ctx")
    dense = dense.reshape(64, -1).astype(F32)
    beside = dense[:, 2 * D : LAST]
    g_router = beside.reshape(64, N_SHARD, 8)[..., :2].reshape(64, E)
    return (
        layer_out.reshape(hidden_in.shape),
        grad_input.reshape(hidden_in.shape),
        beside[:, 2],
        dense[:, 0:D],
        separate(dense[:, D : 2 * D]),
        beside[:, 3],
        beside[0:32, 4],
        dense[:, LAST:],
        beside[:, 5],
        g_router,
        pieces[..., : 2 * FF],
        jnp.swapaxes(pieces[..., 2 * FF :], 1, 2),
    )


def solution(mesh):
    rows = P("shard", "ctx", None)
    flat, line = P("shard", None), P("shard")
    return jax.shard_map(
        local,
        mesh=mesh,
        in_specs=(rows, rows, line, line, flat, flat, line, line, flat, line, flat, rows, P("shard", None, "ctx"), rows),
        out_specs=(rows, rows, line, flat, flat, line, line, flat, line, flat, rows, P("shard", None, "ctx")),
        check_vma=False,
    )
```

```python
import functools

import jax
import jax.numpy as jnp
from jax import lax
from jax.experimental import pallas as pl
from jax.experimental.pallas import tpu as pltpu
from jax.sharding import PartitionSpec as P

D = 1024
KVH = 8
HD = 64
FF = 512
E = 32
SEQ_LEN = 1024
BLK = 128
SEQS = 2
ROWS = SEQS * BLK
CAP = 48
SLOTS = 4 * CAP
N_SHARD = 16
N_CTX = 8
PAIRS = 8
LANE = 128
QB = 256
EPSILON = 1e-06
ROPE_BASE = 10000.0
MASKED = -1e30
F32 = jnp.float32
BF16 = jnp.bfloat16

LANES = [[c + 2 * k for k in range(PAIRS)] for c in range(2)]
CHIPS = [[(c + 2 * k) * N_CTX + j for k in range(PAIRS) for j in range(N_CTX)] for c in range(2)]
OTHER_CORE = [(i, i ^ 1) for i in range(N_SHARD)]
X_LO = [(i, i ^ 2) for i in range(N_SHARD)]
COLUMNS = [[4 * z + 2 * a + c for z in range(4) for c in range(2)] for a in range(2)]
X_HI = [(i, i ^ 4) for i in range(N_CTX)]
SMALL = 3 * D
LAST = 2 * D + LANE


def y_shift(step):
    return [(i, i // 4 * 4 + (i + step) % 4) for i in range(N_CTX)]


def dot(a, b):
    return jnp.dot(a, b, preferred_element_type=F32)


def dot_nt(a, b):
    return lax.dot_general(a, b, (((1,), (1,)), ((), ())), preferred_element_type=F32)


def dot_tn(a, b):
    return lax.dot_general(a, b, (((0,), (0,)), ((), ())), preferred_element_type=F32)


def lane_of(shape):
    return lax.broadcasted_iota(jnp.int32, shape, len(shape) - 1)


def inverse_scale(z):
    return lax.rsqrt(jnp.mean(z * z, axis=-1, keepdims=True) + EPSILON)


def swap_halves(x):
    first = lane_of(x.shape) % HD < HD // 2
    return jnp.where(first, pltpu.roll(x, LANE - HD // 2, 1), pltpu.roll(x, HD // 2, 1))


def side(h):
    return slice(h * LANE, (h + 1) * LANE)


def kernel_call(body, out, flops=0, nbytes=0, mb=48, **kwargs):
    return pl.pallas_call(
        body,
        out_shape=out,
        compiler_params=pltpu.CompilerParams(vmem_limit_bytes=mb * 2**20),
        cost_estimate=pl.CostEstimate(flops=flops, bytes_accessed=nbytes, transcendentals=0),
        **kwargs,
    )


def struct(shape, dtype):
    return jax.ShapeDtypeStruct(shape, dtype)


def key_lanes(shape):
    return lane_of(shape) % LANE < HD


def kv_scale(kv_raw):
    keys = key_lanes(kv_raw.shape)
    total = jnp.sum(jnp.where(keys, kv_raw * kv_raw, 0.0), axis=-1, keepdims=True)
    return lax.rsqrt(total / (D // 2) + EPSILON), keys


def turned_gains(block):
    rows = block.astype(F32).T[0:8]
    place = lane_of(rows.shape) % LANE
    keys = jnp.where(place < HD // 2, rows, pltpu.roll(rows, D - HD // 2, 1))
    keys = jnp.where(place < HD, keys, 1.0)
    which = lax.broadcasted_iota(jnp.int32, rows.shape, 0)
    return jnp.where(which == 2, keys, rows)


def front_body(
    me_ref, x_ref, wq_ref, wkv_ref, small_ref, rope_ref,
    packed_ref, normed_ref, q_ref, kv_ref, gains_ref, w_ref, router_ref, beside_ref,
):
    column = lax.rem(me_ref[0] // 2, 2)
    for z in range(4):
        for a in range(2):
            j = lax.rem(column + a, 2)
            for c in range(2):
                at = slice((4 * z + 2 * a + c) * 64, (4 * z + 2 * a + c + 1) * 64)
                w_ref[at, 0:D] = wq_ref[z, c, j]
                w_ref[at, D : 2 * D] = wkv_ref[z, c, j]
                beside_ref[at] = small_ref[z, c, j]
    router_ref[...] = beside_ref[:, 0:LANE]
    x = x_ref[...].astype(F32)
    gains = turned_gains(beside_ref[:, LANE:])
    gains_ref[...] = gains
    normed = (x * inverse_scale(x) * gains[0:1]).astype(BF16)
    normed_ref[...] = normed
    q = dot(normed, w_ref[:, 0:D])
    kv = dot(normed, w_ref[:, D : 2 * D])
    q_ref[...] = q
    kv_ref[...] = kv
    r_k, keys = kv_scale(kv)
    qn = q * inverse_scale(q) * gains[1:2]
    kn = kv * jnp.where(keys, r_k * gains[2:3], 1.0)
    c, s, ck, sk = rope_ref[0], rope_ref[1], rope_ref[2], rope_ref[3]
    for h in range(KVH):
        qh, kh = qn[:, side(h)], kn[:, side(h)]
        packed_ref[h, :, 0:LANE] = (qh * c + swap_halves(qh) * s).astype(BF16)
        packed_ref[h, :, LANE : 2 * LANE] = (kh * ck + swap_halves(kh) * sk).astype(BF16)


def weight_block(width, at):
    return pl.BlockSpec((4, 2, 2, 64, width), lambda i: (0, 0, 0, 0, at))


def front(places, x, first, rope):
    return kernel_call(
        front_body,
        (
            struct((KVH, ROWS, 2 * LANE), BF16),
            struct((ROWS, D), BF16),
            struct((ROWS, D), F32),
            struct((ROWS, D), F32),
            struct((8, D), F32),
            struct((D, 2 * D), BF16),
            struct((D, LANE), BF16),
        ),
        flops=2 * ROWS * D * 2 * D,
        nbytes=14 * 2**20,
        grid=(1,),
        in_specs=[
            pl.BlockSpec(memory_space=pltpu.SMEM),
            pl.BlockSpec((ROWS, D), lambda i: (0, 0)),
            weight_block(D, 1),
            weight_block(D, 2),
            weight_block(2 * LANE, SMALL // (2 * LANE)),
            pl.BlockSpec((4, ROWS, LANE), lambda i: (0, 0, 0)),
        ],
        scratch_shapes=[pltpu.VMEM((D, 2 * LANE), BF16)],
    )(places, x, first, first, first, rope)


def key_extent(qb):
    return max((qb + 1) * QB, SEQ_LEN // 2)


def both_halves(kv):
    kv = kv.astype(F32)
    turned = pltpu.roll(kv, HD, 1)
    low = lane_of(kv.shape) < HD
    return jnp.where(low, kv, turned).astype(BF16), jnp.where(low, turned, kv).astype(BF16)


def attend_body(prefix_ref, in_ref, out_ref):
    length = prefix_ref[pl.program_id(0)]
    rows = in_ref[...].reshape(SEQ_LEN, 2 * LANE)
    q = rows[:, :LANE] * jnp.asarray(HD**-0.5, BF16)
    k2, v2 = both_halves(rows[:, LANE:])
    group = lane_of((SEQ_LEN, LANE)) // HD
    zero = jnp.zeros((), BF16)
    values = [jnp.where(group == g, v2, zero) for g in range(2)]
    for qb in range(SEQ_LEN // QB):
        lo, hi = qb * QB, key_extent(qb)
        i = lo + lax.broadcasted_iota(jnp.int32, (QB, hi - lo), 0)
        j = lo + lane_of((QB, hi - lo))
        seen = (j <= i) | (j < length)
        total = jnp.zeros((QB, LANE), F32)
        for g in range(2):
            qg = jnp.where(group[lo : lo + QB] == g, q[lo : lo + QB], zero)
            near = jnp.where(seen, dot_nt(qg, k2[lo:hi]), MASKED)
            peak = jnp.max(near, axis=1, keepdims=True)
            if lo:
                far = dot_nt(qg, k2[:lo])
                peak = jnp.maximum(peak, jnp.max(far, axis=1, keepdims=True))
            near = jnp.exp(near - peak)
            norm = jnp.sum(near, axis=1, keepdims=True)
            out = dot(near.astype(BF16), values[g][lo:hi])
            if lo:
                far = jnp.exp(far - peak)
                norm = norm + jnp.sum(far, axis=1, keepdims=True)
                out = out + dot(far.astype(BF16), values[g][:lo])
            total = total + out / norm
        out_ref[2 * qb : 2 * qb + 2] = total.astype(BF16).reshape(2, BLK, LANE)


def attend(prefix, rows):
    return kernel_call(
        attend_body,
        struct((N_CTX, ROWS, LANE), BF16),
        flops=2 * 2 * 2 * 1024 * 1024 * 128,
        nbytes=2 * 2**20,
        grid=(SEQS,),
        in_specs=[
            pl.BlockSpec(memory_space=pltpu.SMEM),
            pl.BlockSpec((N_CTX, BLK, 2 * LANE), lambda s: (0, s, 0)),
        ],
        out_specs=pl.BlockSpec((N_CTX, BLK, LANE), lambda s: (0, s, 0)),
    )(prefix, rows)


def attend_back_body(seq, prefix_ref, in_ref, grad_ref, out_ref, dk_ref, dv_ref):
    length = prefix_ref[seq]
    rows = in_ref[...].reshape(SEQ_LEN, 2 * LANE)
    q = rows[:, :LANE] * jnp.asarray(HD**-0.5, BF16)
    k2, v2 = both_halves(rows[:, LANE:])
    grad = grad_ref[...].reshape(SEQ_LEN, LANE)
    group = lane_of((SEQ_LEN, LANE)) // HD
    zero = jnp.zeros((), BF16)
    keys = [jnp.where(group == g, k2, zero) for g in range(2)]
    dk_ref[...] = jnp.zeros_like(dk_ref)
    dv_ref[...] = jnp.zeros_like(dv_ref)
    for qb in range(SEQ_LEN // QB):
        lo, hi = qb * QB, key_extent(qb)
        i = lo + lane_of((hi - lo, QB))
        j = lo + lax.broadcasted_iota(jnp.int32, (hi - lo, QB), 0)
        seen = (j <= i) | (j < length)
        dq = jnp.zeros((QB, LANE), F32)
        for g in range(2):
            mine = group[lo : lo + QB] == g
            qg = jnp.where(mine, q[lo : lo + QB], zero)
            gg = jnp.where(mine, grad[lo : lo + QB], zero)
            spans = [(lo, hi)] + ([(0, lo)] if lo else [])
            scores = [dot_nt(k2[a:b], qg) for a, b in spans]
            scores[0] = jnp.where(seen, scores[0], MASKED)
            peak = functools.reduce(jnp.maximum, [jnp.max(s, axis=0, keepdims=True) for s in scores])
            scores = [jnp.exp(s - peak) for s in scores]
            norm = 1.0 / sum(jnp.sum(s, axis=0, keepdims=True) for s in scores)
            scores = [s * norm for s in scores]
            grads = [dot_nt(v2[a:b], gg) for a, b in spans]
            inner = sum(jnp.sum(s * d, axis=0, keepdims=True) for s, d in zip(scores, grads))
            for (a, b), s, d in zip(spans, scores, grads):
                ds = (s * (d - inner)).astype(BF16)
                dv_ref[a:b] += dot(s.astype(BF16), gg)
                dk_ref[a:b] += dot(ds, qg)
                dq = dq + dot_tn(ds, keys[g][a:b])
        out_ref[2 * qb : 2 * qb + 2, :, 0:LANE] = (dq * HD**-0.5).astype(BF16).reshape(2, BLK, LANE)
    dk = dk_ref[...]
    dv = dv_ref[...]
    dk = dk + pltpu.roll(dk, HD, 1)
    dv = dv + pltpu.roll(dv, HD, 1)
    out = jnp.where(lane_of(dk.shape) < HD, dk, dv).astype(BF16)
    out_ref[:, :, LANE : 2 * LANE] = out.reshape(N_CTX, BLK, LANE)


def attend_back(seq, prefix, rows, grad):
    return kernel_call(
        functools.partial(attend_back_body, seq),
        struct((N_CTX, BLK, 2 * LANE), BF16),
        flops=5 * 2 * 1024 * 1024 * 128,
        nbytes=2 * 2**20,
        grid=(1,),
        in_specs=[
            pl.BlockSpec(memory_space=pltpu.SMEM),
            pl.BlockSpec((N_CTX, BLK, 2 * LANE), lambda i: (0, seq, 0)),
            pl.BlockSpec((N_CTX, BLK, LANE), lambda i: (0, 0, 0)),
        ],
        out_specs=pl.BlockSpec((N_CTX, BLK, 2 * LANE), lambda i: (0, 0, 0)),
        scratch_shapes=[pltpu.VMEM((SEQ_LEN, LANE), F32), pltpu.VMEM((SEQ_LEN, LANE), F32)],
    )(prefix, rows, grad)


def middle_body(me_ref, x_ref, att_ref, wo_ref, gains_ref, residual_ref, attended_ref, in_ref, *whole_ref):
    for h in range(KVH):
        attended_ref[:, side(h)] = att_ref[h]
    if whole_ref:
        column = lax.rem(me_ref[0] // 2, 2)
        for z in range(4):
            for a in range(2):
                for c in range(2):
                    at = slice((4 * z + 2 * a + c) * 64, (4 * z + 2 * a + c + 1) * 64)
                    whole_ref[0][at] = wo_ref[z, c, lax.rem(column + a, 2)]
        wo = whole_ref[0][...]
    else:
        wo = wo_ref[...]
    residual = x_ref[...].astype(F32) + dot(attended_ref[...], wo)
    residual_ref[...] = residual
    in_ref[...] = (residual * inverse_scale(residual) * gains_ref[3:4]).astype(BF16)


def middle(seq, places, x, att, wo, gains):
    full = lambda *shape: pl.BlockSpec(shape, lambda i: (0,) * len(shape))
    turns = wo.ndim > 2
    return kernel_call(
        middle_body,
        (struct((BLK, D), F32), struct((BLK, D), BF16), struct((BLK, D), BF16))
        + (struct((D, D), BF16),) * turns,
        flops=2 * BLK * D * D,
        nbytes=5 * 2**20,
        grid=(1,),
        in_specs=[
            pl.BlockSpec(memory_space=pltpu.SMEM),
            pl.BlockSpec((BLK, D), lambda i: (seq, 0)),
            pl.BlockSpec((KVH, BLK, LANE), lambda i: (0, seq, 0)),
            weight_block(D, 0) if turns else full(D, D),
            full(8, D),
        ],
        out_specs=(full(BLK, D),) * 3 + (full(D, D),) * turns,
    )(places, x, att, wo, gains)


def softmax_over(logits, member):
    logits = jnp.where(member, logits, MASKED)
    e = jnp.exp(logits - jnp.max(logits, axis=-1, keepdims=True))
    return e / jnp.sum(e, axis=-1, keepdims=True)


def split_two(v):
    high = v.astype(BF16)
    return high, (v - high.astype(F32)).astype(BF16)


def experts_body(seq, me_ref, x_ref, g_ref, slot_ref, router_ref, *refs):
    pieces, refs = refs[:8], refs[8 + 5 * seq :]
    back_refs, refs = refs[: 1 + seq], refs[1 + seq :]
    out_ref, xr_ref, go_ref, mid_ref, dgu_ref = refs[:5]
    wo_ref, gd_ref, gr_ref, w_ref, sem = refs[5:]
    shard = me_ref[0]
    core = lax.rem(shard, 2)

    def weight_copies():
        for n, piece in enumerate(pieces):
            at = pl.multiple_of(me_ref[1 + n] * BLK, BLK)
            for e in range(2):
                yield pltpu.make_async_copy(piece.at[e], w_ref.at[e, pl.ds(at, BLK)], sem.at[2 * n + e])

    @pl.when(pl.program_id(0) == 0)
    def _():
        for copy in weight_copies():
            copy.start()

    cores = (core, 1 - core)
    column = lax.rem(shard // 2, 2)
    chips = [(z, lax.rem(column + a, 2)) for z in range(2) for a in range(2)]
    picks = []
    for k, (z, j) in enumerate(chips):
        want = lax.broadcasted_iota(jnp.int32, (2 * CAP, ROWS), 0).astype(F32)
        pick = []
        for e in range(2):
            near, far = (slot_ref[z, c, j, e : e + 1, seq * BLK : (seq + 1) * BLK] for c in cores)
            slots = jnp.concatenate([near, jnp.where(far < 0, far, far + CAP)], axis=1)
            pick.append((slots == want).astype(F32))
        pick = jnp.concatenate(pick, axis=0).astype(BF16)
        picks.append(pick)
        x = jnp.concatenate([x_ref[z, c, j] for c in cores], axis=0)
        sent = jnp.concatenate([g_ref[z, c, j] for c in cores], axis=0)
        gates = softmax_over(dot(x, router_ref[...]), sent[:, D:].astype(F32) > 0)
        high, low = split_two(gates)
        at = dot(pick, high) + dot(pick, low)
        lane = lane_of(at.shape) - shard * 8
        expert = lax.broadcasted_iota(jnp.int32, at.shape, 0) // (2 * CAP)
        gate = jnp.sum(jnp.where(lane == expert, at, 0.0), axis=-1, keepdims=True)
        rows = dot(pick, x).astype(BF16)
        grad_rows = dot(pick, sent[:, :D])
        scaled = (gate * grad_rows).astype(BF16)
        grad_rows = grad_rows.astype(BF16)
        place = slice(k * 2 * CAP, (k + 1) * 2 * CAP)
        for e in range(2):
            part = slice(e * 2 * CAP, (e + 1) * 2 * CAP)
            xr_ref[e, place] = rows[part]
            go_ref[e, place] = scaled[part]
            gr_ref[e, place] = grad_rows[part]
            gd_ref[e, place] = jnp.broadcast_to(gate[part], (2 * CAP, LANE))

    @pl.when(pl.program_id(0) == 0)
    def _():
        for copy in weight_copies():
            copy.wait()

    dots = []
    for e in range(2):
        gate_up = dot(xr_ref[e], w_ref[e, :, 0 : 2 * FF])
        g, u = gate_up[:, :FF], gate_up[:, FF:]
        sig = 1.0 / (1.0 + jnp.exp(-g))
        act = g * sig
        mid = (act * u).astype(BF16)
        mid_ref[e] = mid
        out = dot_nt(mid, w_ref[e, :, 2 * FF :]).astype(BF16).astype(F32)
        dots.append(jnp.sum(out * gr_ref[e].astype(F32), axis=-1, keepdims=True))
        wo_ref[e] = (out * gd_ref[e, :, 0:1]).astype(BF16)
        grad_mid = dot(go_ref[e], w_ref[e, :, 2 * FF :])
        dgu_ref[e, :, 0:FF] = (grad_mid * u * sig * (1.0 + g * (1.0 - sig))).astype(BF16)
        dgu_ref[e, :, FF : 2 * FF] = (grad_mid * act).astype(BF16)
        gr_ref[e] = dot_nt(dgu_ref[e], w_ref[e, :, 0 : 2 * FF]).astype(BF16)
    for k, (z, j) in enumerate(chips):
        place = slice(k * 2 * CAP, (k + 1) * 2 * CAP)
        pick = picks[k]
        back = dot_tn(pick, jnp.concatenate([gr_ref[0, place], gr_ref[1, place]], axis=0))
        out = dot_tn(pick, jnp.concatenate([wo_ref[0, place], wo_ref[1, place]], axis=0))
        values = jnp.concatenate([dots[0][place], dots[1][place]], axis=0)
        lane = lane_of((SLOTS, LANE)) - shard * 8
        expert = lax.broadcasted_iota(jnp.int32, (SLOTS, LANE), 0) // (2 * CAP)
        high = values.astype(BF16).astype(F32)
        spread_dots = jnp.where(lane == expert, high, jnp.where(lane == expert + 2, values - high, 0.0))
        grad_gate = dot_tn(pick, spread_dots.astype(BF16))
        for n, c in enumerate(cores):
            part = slice(n * BLK, (n + 1) * BLK)
            ref = back_refs[n].at[k] if seq else back_refs[0].at[z, c, j]
            ref[:, 0:D] = back[part].astype(BF16)
            ref[:, D:] = grad_gate[part].astype(BF16)
            out_ref[z, c, j] = out[part].astype(BF16)


def experts(seq, places, x, sent, slots, router, pieces, earlier=()):
    steps = 2
    per = 2 * 4 * CAP
    half = pl.BlockSpec((4, BLK, D + LANE), lambda i: (i, 0, 0))
    kept = lambda width: pl.BlockSpec((2, per, width), lambda i: (0, steps * seq + i, 0))
    total = SEQS * steps * per
    return kernel_call(
        functools.partial(experts_body, seq),
        ((struct((PAIRS, BLK, D + LANE), BF16),) * 2 if seq else (struct((4, 2, 2, BLK, D + LANE), BF16),))
        + (
            struct((4, 2, 2, ROWS + 64, D), BF16),
            struct((2, total, D), BF16),
            struct((2, total, D), BF16),
            struct((2, total, FF), BF16),
            struct((2, total, 2 * FF), BF16),
        ),
        flops=15 * 10**9,
        nbytes=30 * 2**20,
        mb=60,
        grid=(steps,),
        in_specs=[
            pl.BlockSpec(memory_space=pltpu.SMEM),
            pl.BlockSpec((2, 2, 2, BLK, D), lambda i: (i, 0, 0, 0, 0)),
            pl.BlockSpec((2, 2, 2, BLK, D + LANE), lambda i: (i, 0, 0, seq, 0)),
            pl.BlockSpec((2, 2, 2, 2, ROWS), lambda i: (i, 0, 0, 0, 0)),
            pl.BlockSpec((D, LANE), lambda i: (0, 0)),
        ]
        + [pl.BlockSpec(memory_space=pl.ANY)] * (8 + len(earlier)),
        out_specs=((half,) * 2 if seq else (pl.BlockSpec((2, 2, 2, BLK, D + LANE), lambda i: (i, 0, 0, 0, 0)),))
        + (
            pl.BlockSpec((2, 2, 2, BLK, D), lambda i: (i, 0, 0, seq, 0)),
            kept(D), kept(D), kept(FF), kept(2 * FF),
        ),
        input_output_aliases={13 + n: 1 + seq + n for n in range(len(earlier))},
        scratch_shapes=[
            pltpu.VMEM((2, per, D), BF16),
            pltpu.VMEM((2, per, LANE), F32),
            pltpu.VMEM((2, per, D), BF16),
            pltpu.VMEM((2, D, 3 * FF), BF16),
            pltpu.SemaphoreType.DMA((16,)),
        ],
    )(places, x, sent, slots, router, *pieces, *earlier)


def expert_grads_body(me_ref, xa_ref, xb_ref, ga_ref, gb_ref, mid_ref, dgu_ref, *out_refs):
    rows = jnp.concatenate([xa_ref[0], xb_ref[0]], axis=1)
    grad_gu = dot_tn(rows, dgu_ref[0]).astype(BF16)
    rows = jnp.concatenate([ga_ref[0], gb_ref[0]], axis=1)
    grad_down = dot_tn(rows, mid_ref[0]).astype(BF16)
    for step, out_ref in enumerate(out_refs):

        @pl.when(pl.program_id(0) == step)
        def _():
            for half in range(2):
                part = slice(half * BLK, (half + 1) * BLK)
                out_ref[half, :, 0 : 2 * FF] = grad_gu[part]
                out_ref[half, :, 2 * FF :] = grad_down[part]


def expert_grads(expert, places, rows_in, rows_grad, mid, dgu):
    total = rows_in.shape[1]
    column = lambda half: pl.BlockSpec((1, total, BLK), lambda t, me: (expert, 0, me[1 + 2 * t + half]))
    whole = lambda width: pl.BlockSpec((1, total, width), lambda t, me: (expert, 0, 0))
    piece = (2, BLK, 3 * FF)
    return kernel_call(
        expert_grads_body,
        (struct(piece, BF16),) * 4,
        flops=2 * total * D * 3 * FF,
        nbytes=15 * 2**20,
        grid_spec=pltpu.PrefetchScalarGridSpec(
            num_scalar_prefetch=1,
            grid=(4,),
            in_specs=[column(0), column(1), column(0), column(1), whole(FF), whole(2 * FF)],
            out_specs=(pl.BlockSpec(piece, lambda t, me: (0, 0, 0)),) * 4,
        ),
    )(places, rows_in, rows_in, rows_grad, rows_grad, mid, dgu)


def norm_back(z, r, gain, grad):
    weighted = grad * gain
    inner = jnp.mean(weighted * z, axis=-1, keepdims=True)
    return r * weighted - z * (r * r * r) * inner, jnp.sum(grad * z * r, axis=0, keepdims=True)


def turn_body(
    parts_ref, in_ref, residual_ref, cot_ref, member_ref, router_ref, gains_ref, wo_ref,
    gatt_ref, gres_ref, gattn_ref, glog_ref, ggain_ref,
):
    total = parts_ref[0].astype(F32)
    for n in range(1, parts_ref.shape[0]):
        total = total + parts_ref[n].astype(F32)
    gg = total[:, D:]
    gg = gg + pltpu.roll(gg, LANE - 2, 1)
    gates = softmax_over(dot(in_ref[...], router_ref[...]), member_ref[...].astype(F32) > 0)
    chosen = gates * (gg - jnp.sum(gates * gg, axis=-1, keepdims=True))
    glog = chosen.astype(BF16)
    glog_ref[...] = glog
    grad = total[:, :D] + dot_nt(glog, router_ref[...])
    residual = residual_ref[...]
    gz, ggain = norm_back(residual, inverse_scale(residual), gains_ref[3:4], grad)
    ggain_ref[...] = ggain
    gres = cot_ref[...].astype(F32) + gz
    gres_ref[...] = gres
    gattn = gres.astype(BF16)
    gattn_ref[...] = gattn
    gatt = dot_nt(gattn, wo_ref[...]).astype(BF16)
    for h in range(KVH):
        gatt_ref[h] = gatt[:, side(h)]


def turn(seq, parts, expert_in, residual, cot, member, router, gains, wo):
    full = lambda *shape: pl.BlockSpec(shape, lambda i: (0,) * len(shape))
    mine = lambda width: pl.BlockSpec((BLK, width), lambda i: (seq, 0))
    return kernel_call(
        turn_body,
        (
            struct((KVH, BLK, LANE), BF16),
            struct((BLK, D), F32),
            struct((BLK, D), BF16),
            struct((BLK, LANE), BF16),
            struct((1, D), F32),
        ),
        flops=2 * BLK * D * D,
        nbytes=7 * 2**20,
        grid=(1,),
        in_specs=[
            full(*parts.shape), full(BLK, D), full(BLK, D), mine(D), mine(LANE),
            full(D, LANE), full(8, D), full(D, D),
        ],
        out_specs=(full(KVH, BLK, LANE), full(BLK, D), full(BLK, D), full(BLK, LANE), full(1, D)),
    )(parts, expert_in, residual, cot, member, router, gains, wo)


def finish_body(
    me_ref, rows0_ref, rows1_ref, q_ref, kv_ref, x_ref, normed_ref, gres0_ref, gres1_ref, w_ref, gains_ref, rope_ref,
    side_ref, gain0_ref, gain1_ref, grad_in_ref, keep_ref, give_ref, gq_ref, gk_ref, gw_ref,
):
    core = lax.rem(me_ref[0], 2)
    gains = gains_ref[...]
    c, s, ck, sk = rope_ref[0], rope_ref[1], rope_ref[2], rope_ref[3]
    for h in range(KVH):
        both = jnp.concatenate([rows0_ref[h], rows1_ref[h]], axis=0).astype(F32)
        gh, kh = both[:, 0:LANE], both[:, LANE : 2 * LANE]
        gq_ref[:, side(h)] = gh * c - swap_halves(gh) * s
        gk_ref[:, side(h)] = kh * ck - swap_halves(kh) * sk
    q = q_ref[...]
    gq, gain_q = norm_back(q, inverse_scale(q), gains[1:2], gq_ref[...])
    gq = gq.astype(BF16)
    kv, gkv = kv_ref[...], gk_ref[...]
    r, keys = kv_scale(kv)
    weighted = jnp.where(keys, gkv * gains[2:3], 0.0)
    inner = jnp.sum(weighted * kv, axis=-1, keepdims=True) / (D // 2)
    gk = jnp.where(keys, r * weighted - kv * (r * r * r) * inner, gkv).astype(BF16)
    gain_k = jnp.sum(jnp.where(keys, gkv * kv * r, 0.0), axis=0, keepdims=True)
    normed = normed_ref[...]
    gw_ref[:, :, 0:D] = dot_tn(normed, gq).astype(BF16).reshape(N_SHARD, 64, D)
    gw_ref[:, :, D : 2 * D] = dot_tn(normed, gk).astype(BF16).reshape(N_SHARD, 64, D)
    grad = dot_nt(gq, w_ref[:, 0:D]) + dot_nt(gk, w_ref[:, D : 2 * D])
    x = x_ref[...].astype(F32)
    gx, gain_a = norm_back(x, inverse_scale(x), gains[0:1], grad)
    grad_in_ref[...] = (jnp.concatenate([gres0_ref[...], gres1_ref[...]], axis=0) + gx).astype(BF16)
    zero = jnp.zeros((2, D), F32)
    rows = jnp.concatenate([zero, gain_a, gain_q, gain_k, gain0_ref[...] + gain1_ref[...], zero], axis=0)
    which = lax.broadcasted_iota(jnp.int32, rows.shape, 0)
    place = lane_of(rows.shape) % LANE
    rows = jnp.where((which == 4) & (place >= HD), pltpu.roll(rows, HD // 2, 1), rows)
    rows = jnp.concatenate([rows, jnp.zeros((LANE - 8, D), F32)], axis=0)
    beside = (side_ref[...] + rows.T).astype(BF16)
    gw_ref[:, :, 2 * D : LAST] = beside.reshape(N_SHARD, 64, LANE)
    for k in range(PAIRS):
        keep_ref[k] = gw_ref[2 * k + core]
        give_ref[k] = gw_ref[2 * k + 1 - core]


def finish(places, rows, q, kv, x, normed, gres, first, gains, rope, beside, gain_e):
    vmem = pl.BlockSpec(memory_space=pltpu.VMEM)
    return kernel_call(
        finish_body,
        (struct((ROWS, D), BF16),) + (struct((PAIRS, 64, LAST), BF16),) * 2,
        flops=4 * 2 * ROWS * D * D,
        nbytes=15 * 2**20,
        in_specs=[pl.BlockSpec(memory_space=pltpu.SMEM)] + [vmem] * 14,
        scratch_shapes=[
            pltpu.VMEM((ROWS, D), F32),
            pltpu.VMEM((ROWS, D), F32),
            pltpu.VMEM((N_SHARD, 64, LAST), BF16),
        ],
    )(places, *rows, q, kv, x, normed, *gres, first, gains, rope, beside, *gain_e)


def project_back_body(me_ref, *refs):
    att, gattn, rows, glog = refs[0:2], refs[2:4], refs[4:6], refs[6:8]
    out_ref, beside_ref = refs[9:]
    column = lax.rem(me_ref[0] // 2, 2)
    whole = dot_tn(att[0][...], gattn[0][...]) + dot_tn(att[1][...], gattn[1][...])
    whole = whole.astype(BF16).reshape(N_SHARD, 64, D)
    for z in range(4):
        for a in range(2):
            for c in range(2):
                out_ref[z, c, lax.rem(column + a, 2)] = whole[4 * z + 2 * a + c]
    beside_ref[...] = dot_tn(rows[0][...], glog[0][...]) + dot_tn(rows[1][...], glog[1][...])


def project_back(places, attended, gattn, expert_in, glog, out):
    full = lambda *shape: pl.BlockSpec(shape, lambda i: (0,) * len(shape))
    return kernel_call(
        project_back_body,
        (struct(out.shape, BF16), struct((D, LANE), F32)),
        flops=2 * ROWS * D * D,
        nbytes=6 * 2**20,
        grid=(1,),
        in_specs=[pl.BlockSpec(memory_space=pltpu.SMEM)]
        + [full(BLK, D)] * 6
        + [full(BLK, LANE)] * 2
        + [pl.BlockSpec(memory_space=pl.ANY)],
        out_specs=(
            pl.BlockSpec((4, 2, 2, 64, D), lambda i: (0, 0, 0, ROWS // 64, 0)),
            full(D, LANE),
        ),
        input_output_aliases={9: 0},
    )(places, *attended, *gattn, *expert_in, *glog, out)


def interleave(kv):
    return jnp.swapaxes(kv.reshape(-1, 2, KVH, HD), 1, 2).reshape(-1, D)


def separate(kv):
    return jnp.swapaxes(kv.reshape(-1, KVH, 2, HD), 1, 2).reshape(-1, D)


def spread(per_expert):
    rows = per_expert.shape[0]
    padded = jnp.pad(per_expert.reshape(rows, N_SHARD, 2), ((0, 0), (0, 0), (0, 6)))
    return padded.reshape(rows, LANE)


def rope_tables(ctx):
    half = HD // 2
    positions = ctx * BLK + jnp.arange(BLK, dtype=jnp.int32)
    frequency = ROPE_BASE ** (-2.0 * jnp.arange(half, dtype=F32) / HD)
    angles = positions.astype(F32)[:, None] * frequency[None, :]
    c, s = jnp.cos(angles), jnp.sin(angles)
    c, s = jnp.concatenate([c, c], axis=1), jnp.concatenate([-s, s], axis=1)
    one, zero = jnp.ones_like(c), jnp.zeros_like(c)
    pairs = [(c, c), (s, s), (c, one), (s, zero)]
    tables = jnp.stack([jnp.concatenate(p, axis=1) for p in pairs])
    return jnp.concatenate([tables] * SEQS, axis=1)


def to_every(own, axis):
    count = lax.axis_size(axis)
    copies = jnp.broadcast_to(own[None], (count,) + own.shape)
    return lax.all_to_all(copies, axis, 0, 0, tiled=True)


def with_other_core(keep, give):
    got = lax.ppermute(give, "shard", OTHER_CORE)
    return (keep.astype(F32) + got.astype(F32)).astype(BF16)


def tie(*arrays):
    return lax.optimization_barrier(arrays)


def local(
    hidden_in,
    routes,
    prefix,
    gain_attention,
    w_query,
    w_keyval,
    gain_query,
    gain_key,
    w_output,
    gain_experts,
    w_router,
    w_gate_up,
    w_down,
    cotangent,
):
    shard = lax.axis_index("shard")
    ctx = lax.axis_index("ctx")
    core = shard % 2
    x = hidden_in.reshape(ROWS, D)
    cot = cotangent.reshape(ROWS, D)

    def beside(rows):
        return jnp.stack([rows, lax.ppermute(rows, "shard", X_LO)])

    def column_gather(both):
        whole = lax.all_gather(both, "shard", axis=0, axis_index_groups=COLUMNS)
        return whole.reshape((4, 2) + both.shape)

    key_rows = jnp.pad(gain_key, (0, 32))
    columns = jnp.stack([gain_attention, gain_query, key_rows, gain_experts], axis=1)
    first = beside(
        jnp.concatenate(
            [w_output, w_query, interleave(w_keyval), spread(w_router), jnp.pad(columns, ((0, 0), (0, LANE - 4)))],
            axis=1,
        )
    )

    lanes = jnp.arange(LANE, dtype=jnp.int32)
    named = jnp.where(lanes % 8 < 2, lanes // 8 * 2 + lanes % 8, -1)
    member = jnp.any(routes.reshape(ROWS, -1)[:, :, None] == named, axis=1).astype(BF16)
    sent, _ = tie(jnp.concatenate([cot, member], axis=1), first)
    sent = beside(sent)
    first = column_gather(first)

    own_w = jnp.concatenate([w_gate_up, jnp.swapaxes(w_down, 1, 2)], axis=2)
    up, down, far = (lax.ppermute(own_w, "ctx", y_shift(step)) for step in (1, -1, 2))
    own, _ = tie(own_w, sent)
    other_w = lax.ppermute(own, "ctx", X_HI)
    x, sent, other_w, up, down, far = tie(x, sent, other_w, up, down, far)
    high, low = ctx // 4 * 4, ctx % 4
    sources = []
    for step in (0, -1, 1, 2):
        sources += [high + (low + step) % 4, 4 - high + (low + step) % 4]
    places = jnp.stack([shard, *sources]).astype(jnp.int32)

    sent = column_gather(sent)
    own_member = lax.dynamic_slice(sent, (0, 0, 0, 0, D + 8 * shard), (4, 2, 2, ROWS, 2))
    own_member = own_member.reshape(N_SHARD, SEQS, BLK, 2)
    earlier = jnp.tril(jnp.ones((BLK, BLK), BF16), -1)
    slots = jnp.einsum("ts,nbse->nebt", earlier, own_member, preferred_element_type=F32)
    slots = jnp.where(jnp.transpose(own_member, (0, 3, 1, 2)) > 0, slots, -1.0)
    slots = slots.reshape(4, 2, 2, 2, ROWS)

    rope = rope_tables(ctx)
    packed, normed, q_raw, kv_raw, gains, w_whole, router = front(places, x, first, rope)
    packed = lax.all_to_all(packed, "ctx", 0, 0, tiled=True)
    def by_heads(parts):
        return lax.all_to_all(parts, "ctx", 0, 0, tiled=True)

    def to_lanes(parts):
        return lax.all_to_all(parts, "shard", 0, 0, tiled=True, axis_index_groups=LANES)

    att = by_heads(attend(prefix, packed))
    att, other_w = tie(att, other_w)
    other_up, other_down, other_far = (lax.ppermute(other_w, "ctx", y_shift(step)) for step in (1, -1, 2))
    res_a, attended_a, in_a, wo = middle(0, places, x, att, first, gains)
    all_a = column_gather(beside(in_a))
    res_b, attended_b, in_b = middle(1, places, x, att, wo, gains)
    both_b, other_up, other_down, other_far, slots = tie(beside(in_b), other_up, other_down, other_far, slots)
    all_b = column_gather(both_b)

    pieces = (own_w, other_w, up, other_up, down, other_down, far, other_far)
    back, *saved = experts(0, places, all_a, sent, slots, router, pieces)
    columns = lax.psum_scatter(
        back.reshape(PAIRS, 2 * BLK, -1), "shard", scatter_dimension=0, tiled=True, axis_index_groups=COLUMNS
    )
    columns = columns.reshape(2, BLK, -1)
    parts_a = (columns[0], lax.ppermute(columns[1], "shard", X_LO))
    keep, give, *saved = experts(1, places, all_b, sent, slots, router, pieces, saved)
    both = with_other_core(keep, give)
    out, *saved = saved
    both, saved[0] = tie(both, saved[0])
    parts_b = to_lanes(both)
    own_0, down_0, up_0, far_0 = expert_grads(0, places, *saved)
    saved[0], far_0, down_0 = tie(saved[0], far_0, down_0)
    far_0 = lax.ppermute(far_0, "ctx", y_shift(1))
    down_0 = lax.ppermute(down_0, "ctx", y_shift(-1))
    own_1, down_1, up_1, far_1 = expert_grads(1, places, *saved)
    *parts_a, far_0, down_0, far_1, up_1 = tie(*parts_a, far_0, down_0, far_1, up_1)
    parts_a = jnp.stack(parts_a)
    far_1 = lax.ppermute(far_1, "ctx", y_shift(-1))
    up_1 = lax.ppermute(up_1, "ctx", y_shift(1))
    common = (cot, member, router, gains, wo)
    gatt_a, gres_a, gattn_a, glog_a, gain_a = turn(0, parts_a, in_a, res_a, *common)
    parts_b, gatt_a = tie(parts_b, gatt_a)
    back_a = by_heads(gatt_a)
    gatt_b, gres_b, gattn_b, glog_b, gain_b = turn(1, parts_b, in_b, res_b, *common)
    out, beside_grad = project_back(
        places, (attended_a, attended_b), (gattn_a, gattn_b), (in_a, in_b), (glog_a, glog_b), out
    )
    back_a, gatt_b, out, far_1, up_1 = tie(back_a, gatt_b, out, far_1, up_1)
    up_0 = lax.ppermute((up_0.astype(F32) + far_0.astype(F32)).astype(BF16), "ctx", y_shift(1))
    down_1 = lax.ppermute((down_1.astype(F32) + far_1.astype(F32)).astype(BF16), "ctx", y_shift(-1))
    back_b = by_heads(gatt_b)
    grads_a = attend_back(0, prefix, packed, back_a)
    back_b, grads_a, up_0, down_1 = tie(back_b, grads_a, up_0, down_1)
    rows_a = by_heads(grads_a)
    grads_b = attend_back(1, prefix, packed, back_b)
    sums = [sum(g.astype(F32) for g in parts) for parts in ((own_0, up_0, down_0), (own_1, up_1, down_1))]
    columns = lax.psum_scatter(
        out.reshape(PAIRS, 2, ROWS + 64, D), "shard", scatter_dimension=0, tiled=True, axis_index_groups=COLUMNS
    )
    columns = columns.reshape(2, ROWS + 64, D)
    rows_a, grads_b, *sums = tie(rows_a, grads_b, *sums)
    rows_b = by_heads(grads_b)
    gives = lax.ppermute(jnp.stack([g[1] for g in sums]).astype(BF16), "ctx", X_HI)
    rows_b, columns, gives = tie(rows_b, columns, gives)
    got = lax.ppermute(columns[1], "shard", X_LO)
    grad_input, gw_keep, gw_give = finish(
        places, (rows_a, rows_b), q_raw, kv_raw, x, normed, (gres_a, gres_b), w_whole, gains, rope, beside_grad, (gain_a, gain_b)
    )
    got, gw_keep, gw_give = tie(got, gw_keep, gw_give)
    mine = columns[0].astype(F32) + got.astype(F32)
    g_wo = mine[ROWS:].astype(BF16)
    dense, g_wo = tie(with_other_core(gw_keep, gw_give), g_wo)
    layer_out = (jnp.concatenate([res_a, res_b]) + mine[:ROWS]).astype(BF16)
    g_wo = lax.all_gather(g_wo, "ctx", axis=0).astype(F32).sum(axis=0)
    pieces = jnp.stack([g[0] for g in sums]) + gives.astype(F32)

    dense = dense.reshape(PAIRS * N_CTX, 8, -1)
    dense = lax.all_to_all(dense, ("shard", "ctx"), 0, 0, tiled=True, axis_index_groups=CHIPS)
    dense = dense.astype(F32).sum(axis=0).astype(BF16)
    dense = to_every(dense, "ctx").reshape(64, -1).astype(F32)
    beside_grad = dense[:, 2 * D :]
    g_router = beside_grad.reshape(64, N_SHARD, 8)[..., :2].reshape(64, E)
    return (
        layer_out.reshape(hidden_in.shape),
        grad_input.reshape(hidden_in.shape),
        beside_grad[:, 2],
        dense[:, 0:D],
        separate(dense[:, D : 2 * D]),
        beside_grad[:, 3],
        beside_grad[0:32, 4],
        g_wo,
        beside_grad[:, 5],
        g_router,
        pieces[..., : 2 * FF],
        jnp.swapaxes(pieces[..., 2 * FF :], 1, 2),
    )


def solution(mesh):
    rows = P("shard", "ctx", None)
    flat, line = P("shard", None), P("shard")
    return jax.shard_map(
        local,
        mesh=mesh,
        in_specs=(rows, rows, line, line, flat, flat, line, line, flat, line, flat, rows, P("shard", None, "ctx"), rows),
        out_specs=(rows, rows, line, flat, flat, line, line, flat, line, flat, rows, P("shard", None, "ctx")),
        check_vma=False,
    )
```

```python
import functools

import jax
import jax.numpy as jnp
from jax import lax
from jax.experimental import pallas as pl
from jax.experimental.pallas import tpu as pltpu
from jax.sharding import PartitionSpec as P

D = 1024
KVH = 8
HD = 64
FF = 512
E = 32
SEQ_LEN = 1024
BLK = 128
SEQS = 2
ROWS = SEQS * BLK
CAP = 48
SLOTS = 4 * CAP
N_SHARD = 16
N_CTX = 8
PAIRS = 8
LANE = 128
QB = 256
EPSILON = 1e-06
ROPE_BASE = 10000.0
MASKED = -1e30
F32 = jnp.float32
BF16 = jnp.bfloat16

LANES = [[c + 2 * k for k in range(PAIRS)] for c in range(2)]
CHIPS = [[(c + 2 * k) * N_CTX + j for k in range(PAIRS) for j in range(N_CTX)] for c in range(2)]
OTHER_CORE = [(i, i ^ 1) for i in range(N_SHARD)]
X_LO = [(i, i ^ 2) for i in range(N_SHARD)]
COLUMNS = [[4 * z + 2 * a + c for z in range(4) for c in range(2)] for a in range(2)]
X_HI = [(i, i ^ 4) for i in range(N_CTX)]
SMALL = 3 * D
LAST = 2 * D + LANE


Y_NEAR = [(i, i ^ 1) for i in range(N_CTX)]
Y_OTHER = [(i, i ^ 3) for i in range(N_CTX)]


def y_shift(step):
    return [(i, i // 4 * 4 + (i + step) % 4) for i in range(N_CTX)]


def dot(a, b):
    return jnp.dot(a, b, preferred_element_type=F32)


def dot_nt(a, b):
    return lax.dot_general(a, b, (((1,), (1,)), ((), ())), preferred_element_type=F32)


def dot_tn(a, b):
    return lax.dot_general(a, b, (((0,), (0,)), ((), ())), preferred_element_type=F32)


def lane_of(shape):
    return lax.broadcasted_iota(jnp.int32, shape, len(shape) - 1)


def inverse_scale(z):
    return lax.rsqrt(jnp.mean(z * z, axis=-1, keepdims=True) + EPSILON)


def swap_halves(x):
    first = lane_of(x.shape) % HD < HD // 2
    return jnp.where(first, pltpu.roll(x, LANE - HD // 2, 1), pltpu.roll(x, HD // 2, 1))


def side(h):
    return slice(h * LANE, (h + 1) * LANE)


def kernel_call(body, out, flops=0, nbytes=0, mb=62, **kwargs):
    return pl.pallas_call(
        body,
        out_shape=out,
        compiler_params=pltpu.CompilerParams(vmem_limit_bytes=mb * 2**20),
        cost_estimate=pl.CostEstimate(flops=flops, bytes_accessed=nbytes, transcendentals=0),
        **kwargs,
    )


def struct(shape, dtype):
    return jax.ShapeDtypeStruct(shape, dtype)


def key_lanes(shape):
    return lane_of(shape) % LANE < HD


def kv_scale(kv_raw):
    keys = key_lanes(kv_raw.shape)
    total = jnp.sum(jnp.where(keys, kv_raw * kv_raw, 0.0), axis=-1, keepdims=True)
    return lax.rsqrt(total / (D // 2) + EPSILON), keys


def turned_gains(block):
    rows = block.astype(F32).T[0:8]
    place = lane_of(rows.shape) % LANE
    keys = jnp.where(place < HD // 2, rows, pltpu.roll(rows, D - HD // 2, 1))
    keys = jnp.where(place < HD, keys, 1.0)
    which = lax.broadcasted_iota(jnp.int32, rows.shape, 0)
    return jnp.where(which == 2, keys, rows)


def front_body(
    me_ref, x_ref, wq_ref, wkv_ref, small_ref, rope_ref,
    packed_ref, normed_ref, q_ref, kv_ref, gains_ref, w_ref, router_ref, beside_ref,
):
    column = lax.rem(me_ref[0] // 2, 2)
    for z in range(4):
        for a in range(2):
            j = lax.rem(column + a, 2)
            for c in range(2):
                at = slice((4 * z + 2 * a + c) * 64, (4 * z + 2 * a + c + 1) * 64)
                w_ref[at, 0:D] = wq_ref[z, c, j]
                w_ref[at, D : 2 * D] = wkv_ref[z, c, j]
                beside_ref[at] = small_ref[z, c, j]
    router_ref[...] = beside_ref[:, 0:LANE]
    x = x_ref[...].astype(F32)
    gains = turned_gains(beside_ref[:, LANE:])
    gains_ref[...] = gains
    normed = (x * inverse_scale(x) * gains[0:1]).astype(BF16)
    normed_ref[...] = normed
    q = dot(normed, w_ref[:, 0:D])
    kv = dot(normed, w_ref[:, D : 2 * D])
    q_ref[...] = q
    kv_ref[...] = kv
    r_k, keys = kv_scale(kv)
    qn = q * inverse_scale(q) * gains[1:2]
    kn = kv * jnp.where(keys, r_k * gains[2:3], 1.0)
    c, s, ck, sk = rope_ref[0], rope_ref[1], rope_ref[2], rope_ref[3]
    for h in range(KVH):
        qh, kh = qn[:, side(h)], kn[:, side(h)]
        packed_ref[h, :, 0:LANE] = (qh * c + swap_halves(qh) * s).astype(BF16)
        packed_ref[h, :, LANE : 2 * LANE] = (kh * ck + swap_halves(kh) * sk).astype(BF16)


def weight_block(width, at):
    return pl.BlockSpec((4, 2, 2, 64, width), lambda i: (0, 0, 0, 0, at))


def front(places, x, first, rope):
    return kernel_call(
        front_body,
        (
            struct((KVH, ROWS, 2 * LANE), BF16),
            struct((ROWS, D), BF16),
            struct((ROWS, D), F32),
            struct((ROWS, D), F32),
            struct((8, D), F32),
            struct((D, 2 * D), BF16),
            struct((D, LANE), BF16),
        ),
        mb=48,
        flops=2 * ROWS * D * 2 * D,
        nbytes=14 * 2**20,
        grid=(1,),
        in_specs=[
            pl.BlockSpec(memory_space=pltpu.SMEM),
            pl.BlockSpec((ROWS, D), lambda i: (0, 0)),
            weight_block(D, 1),
            weight_block(D, 2),
            weight_block(2 * LANE, SMALL // (2 * LANE)),
            pl.BlockSpec((4, ROWS, LANE), lambda i: (0, 0, 0)),
        ],
        scratch_shapes=[pltpu.VMEM((D, 2 * LANE), BF16)],
    )(places, x, first, first, first, rope)


def key_extent(qb):
    return max((qb + 1) * QB, SEQ_LEN // 2)


def both_halves(kv):
    kv = kv.astype(F32)
    turned = pltpu.roll(kv, HD, 1)
    low = lane_of(kv.shape) < HD
    return jnp.where(low, kv, turned).astype(BF16), jnp.where(low, turned, kv).astype(BF16)


def attend_body(prefix_ref, in_ref, out_ref):
    length = prefix_ref[pl.program_id(0)]
    rows = in_ref[...].reshape(SEQ_LEN, 2 * LANE)
    q = rows[:, :LANE] * jnp.asarray(HD**-0.5, BF16)
    k2, v2 = both_halves(rows[:, LANE:])
    group = lane_of((SEQ_LEN, LANE)) // HD
    zero = jnp.zeros((), BF16)
    values = [jnp.where(group == g, v2, zero) for g in range(2)]
    for qb in range(SEQ_LEN // QB):
        lo, hi = qb * QB, key_extent(qb)
        i = lo + lax.broadcasted_iota(jnp.int32, (QB, hi - lo), 0)
        j = lo + lane_of((QB, hi - lo))
        seen = (j <= i) | (j < length)
        total = jnp.zeros((QB, LANE), F32)
        for g in range(2):
            qg = jnp.where(group[lo : lo + QB] == g, q[lo : lo + QB], zero)
            near = jnp.where(seen, dot_nt(qg, k2[lo:hi]), MASKED)
            peak = jnp.max(near, axis=1, keepdims=True)
            if lo:
                far = dot_nt(qg, k2[:lo])
                peak = jnp.maximum(peak, jnp.max(far, axis=1, keepdims=True))
            near = jnp.exp(near - peak)
            norm = jnp.sum(near, axis=1, keepdims=True)
            out = dot(near.astype(BF16), values[g][lo:hi])
            if lo:
                far = jnp.exp(far - peak)
                norm = norm + jnp.sum(far, axis=1, keepdims=True)
                out = out + dot(far.astype(BF16), values[g][:lo])
            total = total + out / norm
        out_ref[2 * qb : 2 * qb + 2] = total.astype(BF16).reshape(2, BLK, LANE)


def attend(prefix, rows):
    return kernel_call(
        attend_body,
        struct((N_CTX, ROWS, LANE), BF16),
        mb=48,
        flops=2 * 2 * 2 * 1024 * 1024 * 128,
        nbytes=2 * 2**20,
        grid=(SEQS,),
        in_specs=[
            pl.BlockSpec(memory_space=pltpu.SMEM),
            pl.BlockSpec((N_CTX, BLK, 2 * LANE), lambda s: (0, s, 0)),
        ],
        out_specs=pl.BlockSpec((N_CTX, BLK, LANE), lambda s: (0, s, 0)),
    )(prefix, rows)


def attend_back_body(seq, prefix_ref, in_ref, grad_ref, *refs):
    out_ref, dk_ref, dv_ref = refs[seq:]
    length = prefix_ref[seq]
    rows = in_ref[...].reshape(SEQ_LEN, 2 * LANE)
    q = rows[:, :LANE] * jnp.asarray(HD**-0.5, BF16)
    k2, v2 = both_halves(rows[:, LANE:])
    grad = grad_ref[...].reshape(SEQ_LEN, LANE)
    group = lane_of((SEQ_LEN, LANE)) // HD
    zero = jnp.zeros((), BF16)
    keys = [jnp.where(group == g, k2, zero) for g in range(2)]
    dk_ref[...] = jnp.zeros_like(dk_ref)
    dv_ref[...] = jnp.zeros_like(dv_ref)
    for qb in range(SEQ_LEN // QB):
        lo, hi = qb * QB, key_extent(qb)
        i = lo + lane_of((hi - lo, QB))
        j = lo + lax.broadcasted_iota(jnp.int32, (hi - lo, QB), 0)
        seen = (j <= i) | (j < length)
        dq = jnp.zeros((QB, LANE), F32)
        for g in range(2):
            mine = group[lo : lo + QB] == g
            qg = jnp.where(mine, q[lo : lo + QB], zero)
            gg = jnp.where(mine, grad[lo : lo + QB], zero)
            spans = [(lo, hi)] + ([(0, lo)] if lo else [])
            scores = [dot_nt(k2[a:b], qg) for a, b in spans]
            scores[0] = jnp.where(seen, scores[0], MASKED)
            peak = functools.reduce(jnp.maximum, [jnp.max(s, axis=0, keepdims=True) for s in scores])
            scores = [jnp.exp(s - peak) for s in scores]
            norm = 1.0 / sum(jnp.sum(s, axis=0, keepdims=True) for s in scores)
            scores = [s * norm for s in scores]
            grads = [dot_nt(v2[a:b], gg) for a, b in spans]
            inner = sum(jnp.sum(s * d, axis=0, keepdims=True) for s, d in zip(scores, grads))
            for (a, b), s, d in zip(spans, scores, grads):
                ds = (s * (d - inner)).astype(BF16)
                dv_ref[a:b] += dot(s.astype(BF16), gg)
                dk_ref[a:b] += dot(ds, qg)
                dq = dq + dot_tn(ds, keys[g][a:b])
        out_ref[2 * qb : 2 * qb + 2, :, 0:LANE] = (dq * HD**-0.5).astype(BF16).reshape(2, BLK, LANE)
    dk = dk_ref[...]
    dv = dv_ref[...]
    dk = dk + pltpu.roll(dk, HD, 1)
    dv = dv + pltpu.roll(dv, HD, 1)
    out = jnp.where(lane_of(dk.shape) < HD, dk, dv).astype(BF16)
    out_ref[:, :, LANE : 2 * LANE] = out.reshape(N_CTX, BLK, LANE)


def attend_back(seq, prefix, rows, grad, earlier=()):
    return kernel_call(
        functools.partial(attend_back_body, seq),
        struct((N_CTX, ROWS, 2 * LANE), BF16),
        flops=5 * 2 * 1024 * 1024 * 128,
        nbytes=2 * 2**20,
        grid=(1,),
        in_specs=[
            pl.BlockSpec(memory_space=pltpu.SMEM),
            pl.BlockSpec((N_CTX, BLK, 2 * LANE), lambda i: (0, seq, 0)),
            pl.BlockSpec((N_CTX, BLK, LANE), lambda i: (0, 0, 0)),
        ]
        + [pl.BlockSpec(memory_space=pl.ANY)] * len(earlier),
        out_specs=pl.BlockSpec((N_CTX, BLK, 2 * LANE), lambda i: (0, seq, 0)),
        input_output_aliases={3: 0} if earlier else {},
        scratch_shapes=[pltpu.VMEM((SEQ_LEN, LANE), F32), pltpu.VMEM((SEQ_LEN, LANE), F32)],
    )(prefix, rows, grad, *earlier)


def middle_body(me_ref, x_ref, att_ref, wo_ref, gains_ref, residual_ref, attended_ref, in_ref, *whole_ref):
    for h in range(KVH):
        attended_ref[:, side(h)] = att_ref[h]
    if whole_ref:
        column = lax.rem(me_ref[0] // 2, 2)
        for z in range(4):
            for a in range(2):
                for c in range(2):
                    at = slice((4 * z + 2 * a + c) * 64, (4 * z + 2 * a + c + 1) * 64)
                    whole_ref[0][at] = wo_ref[z, c, lax.rem(column + a, 2)]
        wo = whole_ref[0][...]
    else:
        wo = wo_ref[...]
    residual = x_ref[...].astype(F32) + dot(attended_ref[...], wo)
    residual_ref[...] = residual
    in_ref[...] = (residual * inverse_scale(residual) * gains_ref[3:4]).astype(BF16)


def middle(seq, places, x, att, wo, gains):
    full = lambda *shape: pl.BlockSpec(shape, lambda i: (0,) * len(shape))
    turns = wo.ndim > 2
    return kernel_call(
        middle_body,
        (struct((BLK, D), F32), struct((BLK, D), BF16), struct((BLK, D), BF16))
        + (struct((D, D), BF16),) * turns,
        mb=48,
        flops=2 * BLK * D * D,
        nbytes=5 * 2**20,
        grid=(1,),
        in_specs=[
            pl.BlockSpec(memory_space=pltpu.SMEM),
            pl.BlockSpec((BLK, D), lambda i: (seq, 0)),
            pl.BlockSpec((KVH, BLK, LANE), lambda i: (0, seq, 0)),
            weight_block(D, 0) if turns else full(D, D),
            full(8, D),
        ],
        out_specs=(full(BLK, D),) * 3 + (full(D, D),) * turns,
    )(places, x, att, wo, gains)


def softmax_over(logits, member):
    logits = jnp.where(member, logits, MASKED)
    e = jnp.exp(logits - jnp.max(logits, axis=-1, keepdims=True))
    return e / jnp.sum(e, axis=-1, keepdims=True)


def split_two(v):
    high = v.astype(BF16)
    return high, (v - high.astype(F32)).astype(BF16)


def experts_body(seq, me_ref, x_ref, g_ref, slot_ref, router_ref, *refs):
    pieces, refs = refs[:8], refs[8 + 5 * seq :]
    back_ref, out_ref, xr_ref, go_ref, mid_ref, dgu_ref = refs[:6]
    wo_ref, gd_ref, gr_ref, w_ref, sem = refs[6:]
    shard = me_ref[0]
    core = lax.rem(shard, 2)

    def weight_copies():
        for n, piece in enumerate(pieces):
            at = pl.multiple_of(me_ref[1 + n] * BLK, BLK)
            for e in range(2):
                yield pltpu.make_async_copy(piece.at[e], w_ref.at[e, pl.ds(at, BLK)], sem.at[2 * n + e])

    @pl.when(pl.program_id(0) == 0)
    def _():
        for copy in weight_copies():
            copy.start()

    cores = (core, 1 - core)
    column = lax.rem(shard // 2, 2)
    chips = [(z, lax.rem(column + a, 2)) for z in range(2) for a in range(2)]
    picks = []
    for k, (z, j) in enumerate(chips):
        want = lax.broadcasted_iota(jnp.int32, (2 * CAP, ROWS), 0).astype(F32)
        pick = []
        for e in range(2):
            near, far = (slot_ref[z, c, j, e : e + 1, seq * BLK : (seq + 1) * BLK] for c in cores)
            slots = jnp.concatenate([near, jnp.where(far < 0, far, far + CAP)], axis=1)
            pick.append((slots == want).astype(F32))
        pick = jnp.concatenate(pick, axis=0).astype(BF16)
        picks.append(pick)
        x = jnp.concatenate([x_ref[z, c, j] for c in cores], axis=0)
        sent = jnp.concatenate([g_ref[z, c, j] for c in cores], axis=0)
        gates = softmax_over(dot(x, router_ref[...]), sent[:, D:].astype(F32) > 0)
        high, low = split_two(gates)
        at = dot(pick, high) + dot(pick, low)
        lane = lane_of(at.shape) - shard * 8
        expert = lax.broadcasted_iota(jnp.int32, at.shape, 0) // (2 * CAP)
        gate = jnp.sum(jnp.where(lane == expert, at, 0.0), axis=-1, keepdims=True)
        rows = dot(pick, x).astype(BF16)
        grad_rows = dot(pick, sent[:, :D])
        scaled = (gate * grad_rows).astype(BF16)
        grad_rows = grad_rows.astype(BF16)
        place = slice(k * 2 * CAP, (k + 1) * 2 * CAP)
        for e in range(2):
            part = slice(e * 2 * CAP, (e + 1) * 2 * CAP)
            xr_ref[e, place] = rows[part]
            go_ref[e, place] = scaled[part]
            gr_ref[e, place] = grad_rows[part]
            gd_ref[e, place] = jnp.broadcast_to(gate[part], (2 * CAP, LANE))

    @pl.when(pl.program_id(0) == 0)
    def _():
        for copy in weight_copies():
            copy.wait()

    dots = []
    for e in range(2):
        gate_up = dot(xr_ref[e], w_ref[e, :, 0 : 2 * FF])
        g, u = gate_up[:, :FF], gate_up[:, FF:]
        sig = 1.0 / (1.0 + jnp.exp(-g))
        act = g * sig
        mid = (act * u).astype(BF16)
        mid_ref[e] = mid
        out = dot_nt(mid, w_ref[e, :, 2 * FF :]).astype(BF16).astype(F32)
        dots.append(jnp.sum(out * gr_ref[e].astype(F32), axis=-1, keepdims=True))
        wo_ref[e] = (out * gd_ref[e, :, 0:1]).astype(BF16)
        grad_mid = dot(go_ref[e], w_ref[e, :, 2 * FF :])
        dgu_ref[e, :, 0:FF] = (grad_mid * u * sig * (1.0 + g * (1.0 - sig))).astype(BF16)
        dgu_ref[e, :, FF : 2 * FF] = (grad_mid * act).astype(BF16)
        gr_ref[e] = dot_nt(dgu_ref[e], w_ref[e, :, 0 : 2 * FF]).astype(BF16)
    for k, (z, j) in enumerate(chips):
        place = slice(k * 2 * CAP, (k + 1) * 2 * CAP)
        pick = picks[k]
        back = dot_tn(pick, jnp.concatenate([gr_ref[0, place], gr_ref[1, place]], axis=0))
        out = dot_tn(pick, jnp.concatenate([wo_ref[0, place], wo_ref[1, place]], axis=0))
        values = jnp.concatenate([dots[0][place], dots[1][place]], axis=0)
        lane = lane_of((SLOTS, LANE)) - shard * 8
        expert = lax.broadcasted_iota(jnp.int32, (SLOTS, LANE), 0) // (2 * CAP)
        high = values.astype(BF16).astype(F32)
        spread_dots = jnp.where(lane == expert, high, jnp.where(lane == expert + 2, values - high, 0.0))
        grad_gate = dot_tn(pick, spread_dots.astype(BF16))
        for n, c in enumerate(cores):
            part = slice(n * BLK, (n + 1) * BLK)
            back_ref[z, c, j, :, 0:D] = back[part].astype(BF16)
            back_ref[z, c, j, :, D:] = grad_gate[part].astype(BF16)
            out_ref[z, c, j] = out[part].astype(BF16)


def experts(seq, places, x, sent, slots, router, pieces, earlier=()):
    steps = 2
    per = 2 * 4 * CAP
    kept = lambda width: pl.BlockSpec((2, per, width), lambda i: (0, steps * seq + i, 0))
    total = SEQS * steps * per
    return kernel_call(
        functools.partial(experts_body, seq),
        (
            struct((4, 2, 2, BLK, D + LANE), BF16),
            struct((4, 2, 2, ROWS + 64, D), BF16),
            struct((2, total, D), BF16),
            struct((2, total, D), BF16),
            struct((2, total, FF), BF16),
            struct((2, total, 2 * FF), BF16),
        ),
        flops=15 * 10**9,
        nbytes=30 * 2**20,
        mb=60,
        grid=(steps,),
        in_specs=[
            pl.BlockSpec(memory_space=pltpu.SMEM),
            pl.BlockSpec((2, 2, 2, BLK, D), lambda i: (i, 0, 0, 0, 0)),
            pl.BlockSpec((2, 2, 2, BLK, D + LANE), lambda i: (i, 0, 0, seq, 0)),
            pl.BlockSpec((2, 2, 2, 2, ROWS), lambda i: (i, 0, 0, 0, 0)),
            pl.BlockSpec((D, LANE), lambda i: (0, 0)),
        ]
        + [pl.BlockSpec(memory_space=pl.ANY)] * (8 + len(earlier)),
        out_specs=(
            pl.BlockSpec((2, 2, 2, BLK, D + LANE), lambda i: (i, 0, 0, 0, 0)),
            pl.BlockSpec((2, 2, 2, BLK, D), lambda i: (i, 0, 0, seq, 0)),
            kept(D), kept(D), kept(FF), kept(2 * FF),
        ),
        input_output_aliases={13 + n: 1 + n for n in range(len(earlier))},
        scratch_shapes=[
            pltpu.VMEM((2, per, D), BF16),
            pltpu.VMEM((2, per, LANE), F32),
            pltpu.VMEM((2, per, D), BF16),
            pltpu.VMEM((2, D, 3 * FF), BF16),
            pltpu.SemaphoreType.DMA((16,)),
        ],
    )(places, x, sent, slots, router, *pieces, *earlier)


def expert_grads_body(me_ref, xa_ref, xb_ref, ga_ref, gb_ref, mid_ref, dgu_ref, *out_refs):
    rows = jnp.concatenate([xa_ref[0], xb_ref[0]], axis=1)
    grad_gu = dot_tn(rows, dgu_ref[0]).astype(BF16)
    rows = jnp.concatenate([ga_ref[0], gb_ref[0]], axis=1)
    grad_down = dot_tn(rows, mid_ref[0]).astype(BF16)
    for step, out_ref in enumerate(out_refs):

        @pl.when(pl.program_id(0) == step)
        def _():
            for half in range(2):
                part = slice(half * BLK, (half + 1) * BLK)
                out_ref[half, :, 0 : 2 * FF] = grad_gu[part]
                out_ref[half, :, 2 * FF :] = grad_down[part]


def expert_grads(expert, places, rows_in, rows_grad, mid, dgu):
    total = rows_in.shape[1]
    column = lambda half: pl.BlockSpec((1, total, BLK), lambda t, me: (expert, 0, me[1 + 2 * t + half]))
    whole = lambda width: pl.BlockSpec((1, total, width), lambda t, me: (expert, 0, 0))
    piece = (2, BLK, 3 * FF)
    return kernel_call(
        expert_grads_body,
        (struct(piece, BF16),) * 4,
        mb=48,
        flops=2 * total * D * 3 * FF,
        nbytes=15 * 2**20,
        grid_spec=pltpu.PrefetchScalarGridSpec(
            num_scalar_prefetch=1,
            grid=(4,),
            in_specs=[column(0), column(1), column(0), column(1), whole(FF), whole(2 * FF)],
            out_specs=(pl.BlockSpec(piece, lambda t, me: (0, 0, 0)),) * 4,
        ),
    )(places, rows_in, rows_in, rows_grad, rows_grad, mid, dgu)


def norm_back(z, r, gain, grad):
    weighted = grad * gain
    inner = jnp.mean(weighted * z, axis=-1, keepdims=True)
    return r * weighted - z * (r * r * r) * inner, jnp.sum(grad * z * r, axis=0, keepdims=True)


def turn_body(
    mine_ref, got_ref, in_ref, residual_ref, cot_ref, member_ref, router_ref, gains_ref, wo_ref,
    gatt_ref, gres_ref, gattn_ref, glog_ref, ggain_ref,
):
    total = mine_ref[...].astype(F32) + got_ref[...].astype(F32)
    gg = total[:, D:]
    gg = gg + pltpu.roll(gg, LANE - 2, 1)
    gates = softmax_over(dot(in_ref[...], router_ref[...]), member_ref[...].astype(F32) > 0)
    chosen = gates * (gg - jnp.sum(gates * gg, axis=-1, keepdims=True))
    glog = chosen.astype(BF16)
    glog_ref[...] = glog
    grad = total[:, :D] + dot_nt(glog, router_ref[...])
    residual = residual_ref[...]
    gz, ggain = norm_back(residual, inverse_scale(residual), gains_ref[3:4], grad)
    ggain_ref[...] = ggain
    gres = cot_ref[...].astype(F32) + gz
    gres_ref[...] = gres
    gattn = gres.astype(BF16)
    gattn_ref[...] = gattn
    gatt = dot_nt(gattn, wo_ref[...]).astype(BF16)
    for h in range(KVH):
        gatt_ref[h] = gatt[:, side(h)]


def turn(seq, own, got, expert_in, residual, cot, member, router, gains, wo):
    full = lambda *shape: pl.BlockSpec(shape, lambda i: (0,) * len(shape))
    mine = lambda width: pl.BlockSpec((BLK, width), lambda i: (seq, 0))
    return kernel_call(
        turn_body,
        (
            struct((KVH, BLK, LANE), BF16),
            struct((BLK, D), F32),
            struct((BLK, D), BF16),
            struct((BLK, LANE), BF16),
            struct((1, D), F32),
        ),
        flops=2 * BLK * D * D,
        nbytes=7 * 2**20,
        grid=(1,),
        in_specs=[
            full(BLK, D + LANE), full(BLK, D + LANE), full(BLK, D), full(BLK, D), mine(D), mine(LANE),
            full(D, LANE), full(8, D), full(D, D),
        ],
        out_specs=(full(KVH, BLK, LANE), full(BLK, D), full(BLK, D), full(BLK, LANE), full(1, D)),
    )(own, got, expert_in, residual, cot, member, router, gains, wo)


def finish_body(
    me_ref, rows_ref, q_ref, kv_ref, x_ref, normed_ref, gres0_ref, gres1_ref, w_ref, gains_ref, rope_ref,
    side_ref, gain0_ref, gain1_ref, grad_in_ref, keep_ref, give_ref, gq_ref, gk_ref, gw_ref,
):
    core = lax.rem(me_ref[0], 2)
    gains = gains_ref[...]
    c, s, ck, sk = rope_ref[0], rope_ref[1], rope_ref[2], rope_ref[3]
    for h in range(KVH):
        gh = rows_ref[h, :, 0:LANE].astype(F32)
        kh = rows_ref[h, :, LANE : 2 * LANE].astype(F32)
        gq_ref[:, side(h)] = gh * c - swap_halves(gh) * s
        gk_ref[:, side(h)] = kh * ck - swap_halves(kh) * sk
    q = q_ref[...]
    gq, gain_q = norm_back(q, inverse_scale(q), gains[1:2], gq_ref[...])
    gq = gq.astype(BF16)
    kv, gkv = kv_ref[...], gk_ref[...]
    r, keys = kv_scale(kv)
    weighted = jnp.where(keys, gkv * gains[2:3], 0.0)
    inner = jnp.sum(weighted * kv, axis=-1, keepdims=True) / (D // 2)
    gk = jnp.where(keys, r * weighted - kv * (r * r * r) * inner, gkv).astype(BF16)
    gain_k = jnp.sum(jnp.where(keys, gkv * kv * r, 0.0), axis=0, keepdims=True)
    normed = normed_ref[...]
    gw_ref[:, :, 0:D] = dot_tn(normed, gq).astype(BF16).reshape(N_SHARD, 64, D)
    gw_ref[:, :, D : 2 * D] = dot_tn(normed, gk).astype(BF16).reshape(N_SHARD, 64, D)
    grad = dot_nt(gq, w_ref[:, 0:D]) + dot_nt(gk, w_ref[:, D : 2 * D])
    x = x_ref[...].astype(F32)
    gx, gain_a = norm_back(x, inverse_scale(x), gains[0:1], grad)
    grad_in_ref[...] = (jnp.concatenate([gres0_ref[...], gres1_ref[...]], axis=0) + gx).astype(BF16)
    zero = jnp.zeros((2, D), F32)
    rows = jnp.concatenate([zero, gain_a, gain_q, gain_k, gain0_ref[...] + gain1_ref[...], zero], axis=0)
    which = lax.broadcasted_iota(jnp.int32, rows.shape, 0)
    place = lane_of(rows.shape) % LANE
    rows = jnp.where((which == 4) & (place >= HD), pltpu.roll(rows, HD // 2, 1), rows)
    rows = jnp.concatenate([rows, jnp.zeros((LANE - 8, D), F32)], axis=0)
    beside = (side_ref[...] + rows.T).astype(BF16)
    gw_ref[:, :, 2 * D : LAST] = beside.reshape(N_SHARD, 64, LANE)
    for k in range(PAIRS):
        keep_ref[k] = gw_ref[2 * k + core]
        give_ref[k] = gw_ref[2 * k + 1 - core]


def finish(places, rows, q, kv, x, normed, gres, first, gains, rope, beside, gain_e):
    vmem = pl.BlockSpec(memory_space=pltpu.VMEM)
    return kernel_call(
        finish_body,
        (struct((ROWS, D), BF16),) + (struct((PAIRS, 64, LAST), BF16),) * 2,
        flops=4 * 2 * ROWS * D * D,
        nbytes=15 * 2**20,
        in_specs=[pl.BlockSpec(memory_space=pltpu.SMEM)] + [vmem] * 13,
        scratch_shapes=[
            pltpu.VMEM((ROWS, D), F32),
            pltpu.VMEM((ROWS, D), F32),
            pltpu.VMEM((N_SHARD, 64, LAST), BF16),
        ],
    )(places, rows, q, kv, x, normed, *gres, first, gains, rope, beside, *gain_e)


def project_back_body(me_ref, *refs):
    att, gattn, rows, glog = refs[0:2], refs[2:4], refs[4:6], refs[6:8]
    out_ref, beside_ref = refs[9:]
    column = lax.rem(me_ref[0] // 2, 2)
    whole = dot_tn(att[0][...], gattn[0][...]) + dot_tn(att[1][...], gattn[1][...])
    whole = whole.astype(BF16).reshape(N_SHARD, 64, D)
    for z in range(4):
        for a in range(2):
            for c in range(2):
                out_ref[z, c, lax.rem(column + a, 2)] = whole[4 * z + 2 * a + c]
    beside_ref[...] = dot_tn(rows[0][...], glog[0][...]) + dot_tn(rows[1][...], glog[1][...])


def project_back(places, attended, gattn, expert_in, glog, out):
    full = lambda *shape: pl.BlockSpec(shape, lambda i: (0,) * len(shape))
    return kernel_call(
        project_back_body,
        (struct(out.shape, BF16), struct((D, LANE), F32)),
        flops=2 * ROWS * D * D,
        nbytes=6 * 2**20,
        grid=(1,),
        in_specs=[pl.BlockSpec(memory_space=pltpu.SMEM)]
        + [full(BLK, D)] * 6
        + [full(BLK, LANE)] * 2
        + [pl.BlockSpec(memory_space=pl.ANY)],
        out_specs=(
            pl.BlockSpec((4, 2, 2, 64, D), lambda i: (0, 0, 0, ROWS // 64, 0)),
            full(D, LANE),
        ),
        input_output_aliases={9: 0},
    )(places, *attended, *gattn, *expert_in, *glog, out)


def add_body(a_ref, b_ref, c_ref, d_ref, first_ref, second_ref):
    first_ref[...] = (a_ref[...].astype(F32) + b_ref[...].astype(F32)).astype(BF16)
    second_ref[...] = (c_ref[...].astype(F32) + d_ref[...].astype(F32)).astype(BF16)


def add_both(a, b, c, d):
    block = pl.BlockSpec((1,) + a.shape[1:], lambda i: (i, 0, 0))
    return kernel_call(
        add_body,
        (struct(a.shape, BF16),) * 2,
        nbytes=5 * 2**20,
        grid=(a.shape[0],),
        in_specs=[block] * 4,
        out_specs=(block,) * 2,
    )(a, b, c, d)


def prepare_body(wo_ref, wq_ref, wkv_ref, router_ref, gains_ref, out_ref):
    out_ref[:, 0:D] = wo_ref[...]
    out_ref[:, D : 2 * D] = wq_ref[...]
    low = lane_of((64, LANE)) < HD
    for pair in range(KVH // 2):
        k = wkv_ref[:, side(pair)].astype(F32)
        v = wkv_ref[:, side(pair + KVH // 2)].astype(F32)
        even = jnp.where(low, k, pltpu.roll(v, HD, 1))
        odd = jnp.where(low, pltpu.roll(k, HD, 1), v)
        at = 2 * D + 2 * pair * LANE
        out_ref[:, at : at + LANE] = even.astype(BF16)
        out_ref[:, at + LANE : at + 2 * LANE] = odd.astype(BF16)
    expert = lax.broadcasted_iota(jnp.int32, (E, LANE), 0)
    place = (lane_of((E, LANE)) == expert // 2 * 8 + expert % 2).astype(F32).astype(BF16)
    out_ref[:, SMALL : SMALL + LANE] = dot(router_ref[...], place).astype(BF16)
    column = lax.broadcasted_iota(jnp.int32, (8, LANE), 0)
    place = (lane_of((8, LANE)) == column).astype(F32).astype(BF16)
    out_ref[:, SMALL + LANE :] = dot_tn(gains_ref[...], place).astype(BF16)


def prepare(wo, wq, wkv, router, gains):
    return kernel_call(prepare_body, struct((64, SMALL + 2 * LANE), BF16), nbytes=2**20)(wo, wq, wkv, router, gains)


def interleave(kv):
    return jnp.swapaxes(kv.reshape(-1, 2, KVH, HD), 1, 2).reshape(-1, D)


def separate(kv):
    return jnp.swapaxes(kv.reshape(-1, KVH, 2, HD), 1, 2).reshape(-1, D)


def spread(per_expert):
    rows = per_expert.shape[0]
    padded = jnp.pad(per_expert.reshape(rows, N_SHARD, 2), ((0, 0), (0, 0), (0, 6)))
    return padded.reshape(rows, LANE)


def rope_tables(ctx):
    half = HD // 2
    positions = ctx * BLK + jnp.arange(BLK, dtype=jnp.int32)
    frequency = ROPE_BASE ** (-2.0 * jnp.arange(half, dtype=F32) / HD)
    angles = positions.astype(F32)[:, None] * frequency[None, :]
    c, s = jnp.cos(angles), jnp.sin(angles)
    c, s = jnp.concatenate([c, c], axis=1), jnp.concatenate([-s, s], axis=1)
    one, zero = jnp.ones_like(c), jnp.zeros_like(c)
    pairs = [(c, c), (s, s), (c, one), (s, zero)]
    tables = jnp.stack([jnp.concatenate(p, axis=1) for p in pairs])
    return jnp.concatenate([tables] * SEQS, axis=1)


def to_every(own, axis):
    count = lax.axis_size(axis)
    copies = jnp.broadcast_to(own[None], (count,) + own.shape)
    return lax.all_to_all(copies, axis, 0, 0, tiled=True)


def with_other_core(keep, give):
    got = lax.ppermute(give, "shard", OTHER_CORE)
    return (keep.astype(F32) + got.astype(F32)).astype(BF16)


def tie(*arrays):
    return lax.optimization_barrier(arrays)


def local(
    hidden_in,
    routes,
    prefix,
    gain_attention,
    w_query,
    w_keyval,
    gain_query,
    gain_key,
    w_output,
    gain_experts,
    w_router,
    w_gate_up,
    w_down,
    cotangent,
):
    shard = lax.axis_index("shard")
    ctx = lax.axis_index("ctx")
    core = shard % 2
    x = hidden_in.reshape(ROWS, D)
    cot = cotangent.reshape(ROWS, D)

    def beside(rows):
        return jnp.stack([rows, lax.ppermute(rows, "shard", X_LO)])

    def column_gather(both):
        whole = lax.all_gather(both, "shard", axis=0, axis_index_groups=COLUMNS)
        return whole.reshape((4, 2) + both.shape)

    vectors = jnp.stack([gain_attention, gain_query, jnp.pad(gain_key, (0, 32)), gain_experts])
    first = beside(prepare(w_output, w_query, w_keyval, w_router, jnp.pad(vectors, ((0, 4), (0, 0)))))

    lanes = jnp.arange(LANE, dtype=jnp.int32)
    named = jnp.where(lanes % 8 < 2, lanes // 8 * 2 + lanes % 8, -1)
    member = jnp.any(routes.reshape(ROWS, -1)[:, :, None] == named, axis=1).astype(BF16)
    sent, _ = tie(jnp.concatenate([cot, member], axis=1), first)
    sent = beside(sent)
    first = column_gather(first)

    own_w = jnp.concatenate([w_gate_up, jnp.swapaxes(w_down, 1, 2)], axis=2)
    up, down, far = (lax.ppermute(own_w, "ctx", y_shift(step)) for step in (1, -1, 2))
    own, _ = tie(own_w, sent)
    other_w = lax.ppermute(own, "ctx", X_HI)
    x, sent, other_w, up, down, far = tie(x, sent, other_w, up, down, far)
    high, low = ctx // 4 * 4, ctx % 4
    sources = []
    for step in (0, -1, 1, 2):
        sources += [high + (low + step) % 4, 4 - high + (low + step) % 4]
    places = jnp.stack([shard, *sources]).astype(jnp.int32)

    sent = column_gather(sent)
    own_member = lax.dynamic_slice(sent, (0, 0, 0, 0, D + 8 * shard), (4, 2, 2, ROWS, 2))
    own_member = own_member.reshape(N_SHARD, SEQS, BLK, 2)
    earlier = jnp.tril(jnp.ones((BLK, BLK), BF16), -1)
    slots = jnp.einsum("ts,nbse->nebt", earlier, own_member, preferred_element_type=F32)
    slots = jnp.where(jnp.transpose(own_member, (0, 3, 1, 2)) > 0, slots, -1.0)
    slots = slots.reshape(4, 2, 2, 2, ROWS)

    rope = rope_tables(ctx)
    packed, normed, q_raw, kv_raw, gains, w_whole, router = front(places, x, first, rope)
    packed = lax.all_to_all(packed, "ctx", 0, 0, tiled=True)
    def by_heads(parts):
        return lax.all_to_all(parts, "ctx", 0, 0, tiled=True)

    def to_lanes(parts):
        return lax.all_to_all(parts, "shard", 0, 0, tiled=True, axis_index_groups=LANES)

    att = by_heads(attend(prefix, packed))
    att, other_w, far_w = tie(att, other_w, far)
    other_up, other_down = (lax.ppermute(other_w, "ctx", y_shift(step)) for step in (1, -1))
    other_far = lax.ppermute(far_w, "ctx", X_HI)
    res_a, attended_a, in_a, wo = middle(0, places, x, att, first, gains)
    all_a = column_gather(beside(in_a))
    res_b, attended_b, in_b = middle(1, places, x, att, wo, gains)
    both_b, other_up, other_down, other_far, slots = tie(beside(in_b), other_up, other_down, other_far, slots)
    all_b = column_gather(both_b)

    pieces = (own_w, other_w, up, other_up, down, other_down, far, other_far)
    def column_sums(parts):
        columns = lax.psum_scatter(
            parts.reshape(PAIRS, 2 * parts.shape[3], -1),
            "shard",
            scatter_dimension=0,
            tiled=True,
            axis_index_groups=COLUMNS,
        )
        return columns.reshape(2, parts.shape[3], -1)

    def to_neighbour(rows):
        return lax.ppermute(rows, "shard", X_LO)

    common = (cot, member, router, gains, wo)
    back, *saved = experts(0, places, all_a, sent, slots, router, pieces)
    columns_a = column_sums(back)
    back, *saved = experts(1, places, all_b, sent, slots, router, pieces, saved)
    columns_b = column_sums(back)
    out, *saved = saved
    own_0, down_0, up_0, far_0 = expert_grads(0, places, *saved)
    columns_a, saved[0], far_0, down_0 = tie(columns_a, saved[0], far_0, down_0)
    got_a = to_neighbour(columns_a[1])
    far_0 = lax.ppermute(far_0, "ctx", y_shift(1))
    down_0 = lax.ppermute(down_0, "ctx", y_shift(-1))
    own_1, down_1, up_1, far_1 = expert_grads(1, places, *saved)
    got_a, far_1, up_1 = tie(got_a, far_1, up_1)
    far_1 = lax.ppermute(far_1, "ctx", y_shift(-1))
    up_1 = lax.ppermute(up_1, "ctx", y_shift(1))
    gatt_a, gres_a, gattn_a, glog_a, gain_a = turn(0, columns_a[0], got_a, in_a, res_a, *common)
    back_a = by_heads(gatt_a)
    back_a, columns_b, far_0, far_1 = tie(back_a, columns_b, far_0, far_1)
    got_b = to_neighbour(columns_b[1])
    up_0, down_1 = add_both(up_0, far_0, down_1, far_1)
    back_a, up_0, down_1 = tie(back_a, up_0, down_1)
    up_0 = lax.ppermute(up_0, "ctx", y_shift(1))
    down_1 = lax.ppermute(down_1, "ctx", y_shift(-1))
    grads_a = attend_back(0, prefix, packed, back_a)
    got_b, grads_a = tie(got_b, grads_a)
    gatt_b, gres_b, gattn_b, glog_b, gain_b = turn(1, columns_b[0], got_b, in_b, res_b, *common)
    gatt_b, gattn_b = tie(gatt_b, gattn_b)
    back_b = by_heads(gatt_b)
    out, beside_grad = project_back(
        places, (attended_a, attended_b), (gattn_a, gattn_b), (in_a, in_b), (glog_a, glog_b), out
    )
    back_b, out, up_0, down_1, up_1, down_0 = tie(back_b, out, up_0, down_1, up_1, down_0)
    columns = column_sums(out)
    grads = attend_back(1, prefix, packed, back_b, (grads_a,))
    rows = by_heads(grads)
    sums = [sum(g.astype(F32) for g in parts) for parts in ((own_0, up_0, down_0), (own_1, up_1, down_1))]
    gives = jnp.stack([g[1] for g in sums]).astype(BF16)
    gives = lax.ppermute(gives, "ctx", X_HI)
    grad_input, gw_keep, gw_give = finish(
        places, rows, q_raw, kv_raw, x, normed, (gres_a, gres_b), w_whole, gains, rope, beside_grad, (gain_a, gain_b)
    )
    gw_keep, gw_give, gives = tie(gw_keep, gw_give, gives)

    dense = with_other_core(gw_keep, gw_give).reshape(PAIRS * N_CTX, 8, -1)
    dense = lax.all_to_all(dense, ("shard", "ctx"), 0, 0, tiled=True, axis_index_groups=CHIPS)
    got = to_neighbour(columns[1, ROWS:])
    dense, g_wo, got = tie(dense, columns[0, ROWS:], got)
    g_wo = g_wo.astype(F32) + got.astype(F32)
    got = to_neighbour(columns[1, :ROWS])
    for partners in (X_HI, Y_NEAR, Y_OTHER):
        if partners is Y_OTHER:
            g_wo, got = tie(g_wo, got)
        g_wo = g_wo.astype(BF16)
        g_wo = g_wo.astype(F32) + lax.ppermute(g_wo, "ctx", partners).astype(F32)
    dense = to_every(dense.astype(F32).sum(axis=0).astype(BF16), "ctx").reshape(64, -1).astype(F32)
    dense, g_wo = tie(dense, g_wo)
    beside_grad = dense[:, 2 * D :]
    g_router = beside_grad.reshape(64, N_SHARD, 8)[..., :2].reshape(64, E)
    pieces = jnp.stack([g[0] for g in sums]) + gives.astype(F32)

    moe = columns[0, :ROWS].astype(F32) + got.astype(F32)
    layer_out = (jnp.concatenate([res_a, res_b]) + moe).astype(BF16)
    return (
        layer_out.reshape(hidden_in.shape),
        grad_input.reshape(hidden_in.shape),
        beside_grad[:, 2],
        dense[:, 0:D],
        separate(dense[:, D : 2 * D]),
        beside_grad[:, 3],
        beside_grad[0:32, 4],
        g_wo,
        beside_grad[:, 5],
        g_router,
        pieces[..., : 2 * FF],
        jnp.swapaxes(pieces[..., 2 * FF :], 1, 2),
    )


def solution(mesh):
    rows = P("shard", "ctx", None)
    flat, line = P("shard", None), P("shard")
    return jax.shard_map(
        local,
        mesh=mesh,
        in_specs=(rows, rows, line, line, flat, flat, line, line, flat, line, flat, rows, P("shard", None, "ctx"), rows),
        out_specs=(rows, rows, line, flat, flat, line, line, flat, line, flat, rows, P("shard", None, "ctx")),
        check_vma=False,
    )
```

```python
import functools

import jax
import jax.numpy as jnp
from jax import lax
from jax.experimental import pallas as pl
from jax.experimental.pallas import tpu as pltpu
from jax.sharding import PartitionSpec as P

D = 1024
KVH = 8
HD = 64
FF = 512
E = 32
SEQ_LEN = 1024
BLK = 128
SEQS = 2
ROWS = SEQS * BLK
CAP = 48
SLOTS = 4 * CAP
N_SHARD = 16
N_CTX = 8
PAIRS = 8
LANE = 128
QB = 256
EPSILON = 1e-06
ROPE_BASE = 10000.0
MASKED = -1e30
F32 = jnp.float32
BF16 = jnp.bfloat16

LANES = [[c + 2 * k for k in range(PAIRS)] for c in range(2)]
CHIPS = [[(c + 2 * k) * N_CTX + j for k in range(PAIRS) for j in range(N_CTX)] for c in range(2)]
OTHER_CORE = [(i, i ^ 1) for i in range(N_SHARD)]
X_LO = [(i, i ^ 2) for i in range(N_SHARD)]
COLUMNS = [[4 * z + 2 * a + c for z in range(4) for c in range(2)] for a in range(2)]
X_HI = [(i, i ^ 4) for i in range(N_CTX)]
SMALL = 3 * D
LAST = 2 * D + LANE


Y_NEAR = [(i, i ^ 1) for i in range(N_CTX)]
Y_OTHER = [(i, i ^ 3) for i in range(N_CTX)]


def y_shift(step):
    return [(i, i // 4 * 4 + (i + step) % 4) for i in range(N_CTX)]


def dot(a, b):
    return jnp.dot(a, b, preferred_element_type=F32)


def dot_nt(a, b):
    return lax.dot_general(a, b, (((1,), (1,)), ((), ())), preferred_element_type=F32)


def dot_tn(a, b):
    return lax.dot_general(a, b, (((0,), (0,)), ((), ())), preferred_element_type=F32)


def lane_of(shape):
    return lax.broadcasted_iota(jnp.int32, shape, len(shape) - 1)


def inverse_scale(z):
    return lax.rsqrt(jnp.mean(z * z, axis=-1, keepdims=True) + EPSILON)


def swap_halves(x):
    first = lane_of(x.shape) % HD < HD // 2
    return jnp.where(first, pltpu.roll(x, LANE - HD // 2, 1), pltpu.roll(x, HD // 2, 1))


def side(h):
    return slice(h * LANE, (h + 1) * LANE)


def kernel_call(body, out, flops=0, nbytes=0, mb=62, **kwargs):
    return pl.pallas_call(
        body,
        out_shape=out,
        compiler_params=pltpu.CompilerParams(vmem_limit_bytes=mb * 2**20),
        cost_estimate=pl.CostEstimate(flops=flops, bytes_accessed=nbytes, transcendentals=0),
        **kwargs,
    )


def struct(shape, dtype):
    return jax.ShapeDtypeStruct(shape, dtype)


def key_lanes(shape):
    return lane_of(shape) % LANE < HD


def kv_scale(kv_raw):
    keys = key_lanes(kv_raw.shape)
    total = jnp.sum(jnp.where(keys, kv_raw * kv_raw, 0.0), axis=-1, keepdims=True)
    return lax.rsqrt(total / (D // 2) + EPSILON), keys


def turned_gains(block):
    rows = block.astype(F32).T[0:8]
    place = lane_of(rows.shape) % LANE
    keys = jnp.where(place < HD // 2, rows, pltpu.roll(rows, D - HD // 2, 1))
    keys = jnp.where(place < HD, keys, 1.0)
    which = lax.broadcasted_iota(jnp.int32, rows.shape, 0)
    return jnp.where(which == 2, keys, rows)


def front_body(
    me_ref, x_ref, wq_ref, wkv_ref, small_ref, rope_ref,
    packed_ref, normed_ref, q_ref, kv_ref, gains_ref, w_ref, router_ref, beside_ref,
):
    column = lax.rem(me_ref[0] // 2, 2)
    for z in range(4):
        for a in range(2):
            j = lax.rem(column + a, 2)
            for c in range(2):
                at = slice((4 * z + 2 * a + c) * 64, (4 * z + 2 * a + c + 1) * 64)
                w_ref[at, 0:D] = wq_ref[z, c, j]
                w_ref[at, D : 2 * D] = wkv_ref[z, c, j]
                beside_ref[at] = small_ref[z, c, j]
    router_ref[...] = beside_ref[:, 0:LANE]
    x = x_ref[...].astype(F32)
    gains = turned_gains(beside_ref[:, LANE:])
    gains_ref[...] = gains
    normed = (x * inverse_scale(x) * gains[0:1]).astype(BF16)
    normed_ref[...] = normed
    q = dot(normed, w_ref[:, 0:D])
    kv = dot(normed, w_ref[:, D : 2 * D])
    q_ref[...] = q
    kv_ref[...] = kv
    r_k, keys = kv_scale(kv)
    qn = q * inverse_scale(q) * gains[1:2]
    kn = kv * jnp.where(keys, r_k * gains[2:3], 1.0)
    c, s, ck, sk = rope_ref[0], rope_ref[1], rope_ref[2], rope_ref[3]
    for h in range(KVH):
        qh, kh = qn[:, side(h)], kn[:, side(h)]
        packed_ref[h, :, 0:LANE] = (qh * c + swap_halves(qh) * s).astype(BF16)
        packed_ref[h, :, LANE : 2 * LANE] = (kh * ck + swap_halves(kh) * sk).astype(BF16)


def weight_block(width, at):
    return pl.BlockSpec((4, 2, 2, 64, width), lambda i: (0, 0, 0, 0, at))


def front(places, x, first, rope):
    return kernel_call(
        front_body,
        (
            struct((KVH, ROWS, 2 * LANE), BF16),
            struct((ROWS, D), BF16),
            struct((ROWS, D), F32),
            struct((ROWS, D), F32),
            struct((8, D), F32),
            struct((D, 2 * D), BF16),
            struct((D, LANE), BF16),
        ),
        mb=48,
        flops=2 * ROWS * D * 2 * D,
        nbytes=14 * 2**20,
        grid=(1,),
        in_specs=[
            pl.BlockSpec(memory_space=pltpu.SMEM),
            pl.BlockSpec((ROWS, D), lambda i: (0, 0)),
            weight_block(D, 1),
            weight_block(D, 2),
            weight_block(2 * LANE, SMALL // (2 * LANE)),
            pl.BlockSpec((4, ROWS, LANE), lambda i: (0, 0, 0)),
        ],
        scratch_shapes=[pltpu.VMEM((D, 2 * LANE), BF16)],
    )(places, x, first, first, first, rope)


def key_extent(qb):
    return max((qb + 1) * QB, SEQ_LEN // 2)


def both_halves(kv):
    kv = kv.astype(F32)
    turned = pltpu.roll(kv, HD, 1)
    low = lane_of(kv.shape) < HD
    return jnp.where(low, kv, turned).astype(BF16), jnp.where(low, turned, kv).astype(BF16)


def attend_body(prefix_ref, in_ref, out_ref):
    length = prefix_ref[pl.program_id(0)]
    rows = in_ref[...].reshape(SEQ_LEN, 2 * LANE)
    q = rows[:, :LANE] * jnp.asarray(HD**-0.5, BF16)
    k2, v2 = both_halves(rows[:, LANE:])
    group = lane_of((SEQ_LEN, LANE)) // HD
    zero = jnp.zeros((), BF16)
    values = [jnp.where(group == g, v2, zero) for g in range(2)]
    for qb in range(SEQ_LEN // QB):
        lo, hi = qb * QB, key_extent(qb)
        i = lo + lax.broadcasted_iota(jnp.int32, (QB, hi - lo), 0)
        j = lo + lane_of((QB, hi - lo))
        seen = (j <= i) | (j < length)
        total = jnp.zeros((QB, LANE), F32)
        for g in range(2):
            qg = jnp.where(group[lo : lo + QB] == g, q[lo : lo + QB], zero)
            near = jnp.where(seen, dot_nt(qg, k2[lo:hi]), MASKED)
            peak = jnp.max(near, axis=1, keepdims=True)
            if lo:
                far = dot_nt(qg, k2[:lo])
                peak = jnp.maximum(peak, jnp.max(far, axis=1, keepdims=True))
            near = jnp.exp(near - peak)
            norm = jnp.sum(near, axis=1, keepdims=True)
            out = dot(near.astype(BF16), values[g][lo:hi])
            if lo:
                far = jnp.exp(far - peak)
                norm = norm + jnp.sum(far, axis=1, keepdims=True)
                out = out + dot(far.astype(BF16), values[g][:lo])
            total = total + out / norm
        out_ref[2 * qb : 2 * qb + 2] = total.astype(BF16).reshape(2, BLK, LANE)


def attend(prefix, rows):
    return kernel_call(
        attend_body,
        struct((N_CTX, ROWS, LANE), BF16),
        mb=48,
        flops=2 * 2 * 2 * 1024 * 1024 * 128,
        nbytes=2 * 2**20,
        grid=(SEQS,),
        in_specs=[
            pl.BlockSpec(memory_space=pltpu.SMEM),
            pl.BlockSpec((N_CTX, BLK, 2 * LANE), lambda s: (0, s, 0)),
        ],
        out_specs=pl.BlockSpec((N_CTX, BLK, LANE), lambda s: (0, s, 0)),
    )(prefix, rows)


def attend_back_body(seq, prefix_ref, in_ref, grad_ref, *refs):
    out_ref, dk_ref, dv_ref = refs[seq:]
    length = prefix_ref[seq]
    rows = in_ref[...].reshape(SEQ_LEN, 2 * LANE)
    q = rows[:, :LANE] * jnp.asarray(HD**-0.5, BF16)
    k2, v2 = both_halves(rows[:, LANE:])
    grad = grad_ref[...].reshape(SEQ_LEN, LANE)
    group = lane_of((SEQ_LEN, LANE)) // HD
    zero = jnp.zeros((), BF16)
    keys = [jnp.where(group == g, k2, zero) for g in range(2)]
    dk_ref[...] = jnp.zeros_like(dk_ref)
    dv_ref[...] = jnp.zeros_like(dv_ref)
    for qb in range(SEQ_LEN // QB):
        lo, hi = qb * QB, key_extent(qb)
        i = lo + lane_of((hi - lo, QB))
        j = lo + lax.broadcasted_iota(jnp.int32, (hi - lo, QB), 0)
        seen = (j <= i) | (j < length)
        dq = jnp.zeros((QB, LANE), F32)
        for g in range(2):
            mine = group[lo : lo + QB] == g
            qg = jnp.where(mine, q[lo : lo + QB], zero)
            gg = jnp.where(mine, grad[lo : lo + QB], zero)
            spans = [(lo, hi)] + ([(0, lo)] if lo else [])
            scores = [dot_nt(k2[a:b], qg) for a, b in spans]
            scores[0] = jnp.where(seen, scores[0], MASKED)
            peak = functools.reduce(jnp.maximum, [jnp.max(s, axis=0, keepdims=True) for s in scores])
            scores = [jnp.exp(s - peak) for s in scores]
            norm = 1.0 / sum(jnp.sum(s, axis=0, keepdims=True) for s in scores)
            scores = [s * norm for s in scores]
            grads = [dot_nt(v2[a:b], gg) for a, b in spans]
            inner = sum(jnp.sum(s * d, axis=0, keepdims=True) for s, d in zip(scores, grads))
            for (a, b), s, d in zip(spans, scores, grads):
                ds = (s * (d - inner)).astype(BF16)
                dv_ref[a:b] += dot(s.astype(BF16), gg)
                dk_ref[a:b] += dot(ds, qg)
                dq = dq + dot_tn(ds, keys[g][a:b])
        out_ref[2 * qb : 2 * qb + 2, :, 0:LANE] = (dq * HD**-0.5).astype(BF16).reshape(2, BLK, LANE)
    dk = dk_ref[...]
    dv = dv_ref[...]
    dk = dk + pltpu.roll(dk, HD, 1)
    dv = dv + pltpu.roll(dv, HD, 1)
    out = jnp.where(lane_of(dk.shape) < HD, dk, dv).astype(BF16)
    out_ref[:, :, LANE : 2 * LANE] = out.reshape(N_CTX, BLK, LANE)


def attend_back(seq, prefix, rows, grad, earlier=()):
    return kernel_call(
        functools.partial(attend_back_body, seq),
        struct((N_CTX, ROWS, 2 * LANE), BF16),
        flops=5 * 2 * 1024 * 1024 * 128,
        nbytes=2 * 2**20,
        grid=(1,),
        in_specs=[
            pl.BlockSpec(memory_space=pltpu.SMEM),
            pl.BlockSpec((N_CTX, BLK, 2 * LANE), lambda i: (0, seq, 0)),
            pl.BlockSpec((N_CTX, BLK, LANE), lambda i: (0, 0, 0)),
        ]
        + [pl.BlockSpec(memory_space=pl.ANY)] * len(earlier),
        out_specs=pl.BlockSpec((N_CTX, BLK, 2 * LANE), lambda i: (0, seq, 0)),
        input_output_aliases={3: 0} if earlier else {},
        scratch_shapes=[pltpu.VMEM((SEQ_LEN, LANE), F32), pltpu.VMEM((SEQ_LEN, LANE), F32)],
    )(prefix, rows, grad, *earlier)


def middle_body(me_ref, x_ref, att_ref, wo_ref, gains_ref, residual_ref, attended_ref, in_ref, *whole_ref):
    for h in range(KVH):
        attended_ref[:, side(h)] = att_ref[h]
    if whole_ref:
        column = lax.rem(me_ref[0] // 2, 2)
        for z in range(4):
            for a in range(2):
                for c in range(2):
                    at = slice((4 * z + 2 * a + c) * 64, (4 * z + 2 * a + c + 1) * 64)
                    whole_ref[0][at] = wo_ref[z, c, lax.rem(column + a, 2)]
        wo = whole_ref[0][...]
    else:
        wo = wo_ref[...]
    residual = x_ref[...].astype(F32) + dot(attended_ref[...], wo)
    residual_ref[...] = residual
    in_ref[...] = (residual * inverse_scale(residual) * gains_ref[3:4]).astype(BF16)


def middle(seq, places, x, att, wo, gains):
    full = lambda *shape: pl.BlockSpec(shape, lambda i: (0,) * len(shape))
    turns = wo.ndim > 2
    return kernel_call(
        middle_body,
        (struct((BLK, D), F32), struct((BLK, D), BF16), struct((BLK, D), BF16))
        + (struct((D, D), BF16),) * turns,
        mb=48,
        flops=2 * BLK * D * D,
        nbytes=5 * 2**20,
        grid=(1,),
        in_specs=[
            pl.BlockSpec(memory_space=pltpu.SMEM),
            pl.BlockSpec((BLK, D), lambda i: (seq, 0)),
            pl.BlockSpec((KVH, BLK, LANE), lambda i: (0, seq, 0)),
            weight_block(D, 0) if turns else full(D, D),
            full(8, D),
        ],
        out_specs=(full(BLK, D),) * 3 + (full(D, D),) * turns,
    )(places, x, att, wo, gains)


def softmax_over(logits, member):
    logits = jnp.where(member, logits, MASKED)
    e = jnp.exp(logits - jnp.max(logits, axis=-1, keepdims=True))
    return e / jnp.sum(e, axis=-1, keepdims=True)


def split_two(v):
    high = v.astype(BF16)
    return high, (v - high.astype(F32)).astype(BF16)


def experts_body(seq, me_ref, x_ref, g_ref, slot_ref, router_ref, *refs):
    pieces, refs = refs[:8], refs[8 + 5 * seq :]
    back_ref, out_ref, xr_ref, go_ref, mid_ref, dgu_ref = refs[:6]
    wo_ref, gd_ref, gr_ref, w_ref, sem = refs[6:]
    shard = me_ref[0]
    core = lax.rem(shard, 2)

    def weight_copies():
        for n, piece in enumerate(pieces):
            at = pl.multiple_of(me_ref[1 + n] * BLK, BLK)
            for e in range(2):
                yield pltpu.make_async_copy(piece.at[e], w_ref.at[e, pl.ds(at, BLK)], sem.at[2 * n + e])

    @pl.when(pl.program_id(0) == 0)
    def _():
        for copy in weight_copies():
            copy.start()

    cores = (core, 1 - core)
    column = lax.rem(shard // 2, 2)
    chips = [(z, lax.rem(column + a, 2)) for z in range(2) for a in range(2)]
    picks = []
    for k, (z, j) in enumerate(chips):
        want = lax.broadcasted_iota(jnp.int32, (2 * CAP, ROWS), 0).astype(F32)
        pick = []
        for e in range(2):
            near, far = (slot_ref[z, c, j, e : e + 1, seq * BLK : (seq + 1) * BLK] for c in cores)
            slots = jnp.concatenate([near, jnp.where(far < 0, far, far + CAP)], axis=1)
            pick.append((slots == want).astype(F32))
        pick = jnp.concatenate(pick, axis=0).astype(BF16)
        picks.append(pick)
        x = jnp.concatenate([x_ref[z, c, j] for c in cores], axis=0)
        sent = jnp.concatenate([g_ref[z, c, j] for c in cores], axis=0)
        gates = softmax_over(dot(x, router_ref[...]), sent[:, D:].astype(F32) > 0)
        high, low = split_two(gates)
        at = dot(pick, high) + dot(pick, low)
        lane = lane_of(at.shape) - shard * 8
        expert = lax.broadcasted_iota(jnp.int32, at.shape, 0) // (2 * CAP)
        gate = jnp.sum(jnp.where(lane == expert, at, 0.0), axis=-1, keepdims=True)
        rows = dot(pick, x).astype(BF16)
        grad_rows = dot(pick, sent[:, :D])
        scaled = (gate * grad_rows).astype(BF16)
        grad_rows = grad_rows.astype(BF16)
        place = slice(k * 2 * CAP, (k + 1) * 2 * CAP)
        for e in range(2):
            part = slice(e * 2 * CAP, (e + 1) * 2 * CAP)
            xr_ref[e, place] = rows[part]
            go_ref[e, place] = scaled[part]
            gr_ref[e, place] = grad_rows[part]
            gd_ref[e, place] = jnp.broadcast_to(gate[part], (2 * CAP, LANE))

    @pl.when(pl.program_id(0) == 0)
    def _():
        for copy in weight_copies():
            copy.wait()

    dots = []
    for e in range(2):
        gate_up = dot(xr_ref[e], w_ref[e, :, 0 : 2 * FF])
        g, u = gate_up[:, :FF], gate_up[:, FF:]
        sig = 1.0 / (1.0 + jnp.exp(-g))
        act = g * sig
        mid = (act * u).astype(BF16)
        mid_ref[e] = mid
        out = dot_nt(mid, w_ref[e, :, 2 * FF :]).astype(BF16).astype(F32)
        dots.append(jnp.sum(out * gr_ref[e].astype(F32), axis=-1, keepdims=True))
        wo_ref[e] = (out * gd_ref[e, :, 0:1]).astype(BF16)
        grad_mid = dot(go_ref[e], w_ref[e, :, 2 * FF :])
        dgu_ref[e, :, 0:FF] = (grad_mid * u * sig * (1.0 + g * (1.0 - sig))).astype(BF16)
        dgu_ref[e, :, FF : 2 * FF] = (grad_mid * act).astype(BF16)
        gr_ref[e] = dot_nt(dgu_ref[e], w_ref[e, :, 0 : 2 * FF]).astype(BF16)
    for k, (z, j) in enumerate(chips):
        place = slice(k * 2 * CAP, (k + 1) * 2 * CAP)
        pick = picks[k]
        back = dot_tn(pick, jnp.concatenate([gr_ref[0, place], gr_ref[1, place]], axis=0))
        out = dot_tn(pick, jnp.concatenate([wo_ref[0, place], wo_ref[1, place]], axis=0))
        values = jnp.concatenate([dots[0][place], dots[1][place]], axis=0)
        lane = lane_of((SLOTS, LANE)) - shard * 8
        expert = lax.broadcasted_iota(jnp.int32, (SLOTS, LANE), 0) // (2 * CAP)
        high = values.astype(BF16).astype(F32)
        spread_dots = jnp.where(lane == expert, high, jnp.where(lane == expert + 2, values - high, 0.0))
        grad_gate = dot_tn(pick, spread_dots.astype(BF16))
        for n, c in enumerate(cores):
            part = slice(n * BLK, (n + 1) * BLK)
            back_ref[z, c, j, :, 0:D] = back[part].astype(BF16)
            back_ref[z, c, j, :, D:] = grad_gate[part].astype(BF16)
            out_ref[z, c, j] = out[part].astype(BF16)


def experts(seq, places, x, sent, slots, router, pieces, earlier=()):
    steps = 2
    per = 2 * 4 * CAP
    kept = lambda width: pl.BlockSpec((2, per, width), lambda i: (0, steps * seq + i, 0))
    total = SEQS * steps * per
    return kernel_call(
        functools.partial(experts_body, seq),
        (
            struct((4, 2, 2, BLK, D + LANE), BF16),
            struct((4, 2, 2, ROWS + 64, D), BF16),
            struct((2, total, D), BF16),
            struct((2, total, D), BF16),
            struct((2, total, FF), BF16),
            struct((2, total, 2 * FF), BF16),
        ),
        flops=15 * 10**9,
        nbytes=30 * 2**20,
        mb=60,
        grid=(steps,),
        in_specs=[
            pl.BlockSpec(memory_space=pltpu.SMEM),
            pl.BlockSpec((2, 2, 2, BLK, D), lambda i: (i, 0, 0, 0, 0)),
            pl.BlockSpec((2, 2, 2, BLK, D + LANE), lambda i: (i, 0, 0, seq, 0)),
            pl.BlockSpec((2, 2, 2, 2, ROWS), lambda i: (i, 0, 0, 0, 0)),
            pl.BlockSpec((D, LANE), lambda i: (0, 0)),
        ]
        + [pl.BlockSpec(memory_space=pl.ANY)] * (8 + len(earlier)),
        out_specs=(
            pl.BlockSpec((2, 2, 2, BLK, D + LANE), lambda i: (i, 0, 0, 0, 0)),
            pl.BlockSpec((2, 2, 2, BLK, D), lambda i: (i, 0, 0, seq, 0)),
            kept(D), kept(D), kept(FF), kept(2 * FF),
        ),
        input_output_aliases={13 + n: 1 + n for n in range(len(earlier))},
        scratch_shapes=[
            pltpu.VMEM((2, per, D), BF16),
            pltpu.VMEM((2, per, LANE), F32),
            pltpu.VMEM((2, per, D), BF16),
            pltpu.VMEM((2, D, 3 * FF), BF16),
            pltpu.SemaphoreType.DMA((16,)),
        ],
    )(places, x, sent, slots, router, *pieces, *earlier)


def expert_grads_body(me_ref, xa_ref, xb_ref, ga_ref, gb_ref, mid_ref, dgu_ref, *out_refs):
    rows = jnp.concatenate([xa_ref[0], xb_ref[0]], axis=1)
    grad_gu = dot_tn(rows, dgu_ref[0]).astype(BF16)
    rows = jnp.concatenate([ga_ref[0], gb_ref[0]], axis=1)
    grad_down = dot_tn(rows, mid_ref[0]).astype(BF16)
    for step, out_ref in enumerate(out_refs):

        @pl.when(pl.program_id(0) == step)
        def _():
            for half in range(2):
                part = slice(half * BLK, (half + 1) * BLK)
                out_ref[half, :, 0 : 2 * FF] = grad_gu[part]
                out_ref[half, :, 2 * FF :] = grad_down[part]


def expert_grads(expert, places, rows_in, rows_grad, mid, dgu):
    total = rows_in.shape[1]
    column = lambda half: pl.BlockSpec((1, total, BLK), lambda t, me: (expert, 0, me[1 + 2 * t + half]))
    whole = lambda width: pl.BlockSpec((1, total, width), lambda t, me: (expert, 0, 0))
    piece = (2, BLK, 3 * FF)
    return kernel_call(
        expert_grads_body,
        (struct(piece, BF16),) * 4,
        mb=48,
        flops=2 * total * D * 3 * FF,
        nbytes=15 * 2**20,
        grid_spec=pltpu.PrefetchScalarGridSpec(
            num_scalar_prefetch=1,
            grid=(4,),
            in_specs=[column(0), column(1), column(0), column(1), whole(FF), whole(2 * FF)],
            out_specs=(pl.BlockSpec(piece, lambda t, me: (0, 0, 0)),) * 4,
        ),
    )(places, rows_in, rows_in, rows_grad, rows_grad, mid, dgu)


def norm_back(z, r, gain, grad):
    weighted = grad * gain
    inner = jnp.mean(weighted * z, axis=-1, keepdims=True)
    return r * weighted - z * (r * r * r) * inner, jnp.sum(grad * z * r, axis=0, keepdims=True)


def turn_body(
    mine_ref, got_ref, in_ref, residual_ref, cot_ref, member_ref, router_ref, gains_ref, wo_ref,
    gatt_ref, gres_ref, gattn_ref, glog_ref, ggain_ref,
):
    total = mine_ref[...].astype(F32) + got_ref[...].astype(F32)
    gg = total[:, D:]
    gg = gg + pltpu.roll(gg, LANE - 2, 1)
    gates = softmax_over(dot(in_ref[...], router_ref[...]), member_ref[...].astype(F32) > 0)
    chosen = gates * (gg - jnp.sum(gates * gg, axis=-1, keepdims=True))
    glog = chosen.astype(BF16)
    glog_ref[...] = glog
    grad = total[:, :D] + dot_nt(glog, router_ref[...])
    residual = residual_ref[...]
    gz, ggain = norm_back(residual, inverse_scale(residual), gains_ref[3:4], grad)
    ggain_ref[...] = ggain
    gres = cot_ref[...].astype(F32) + gz
    gres_ref[...] = gres
    gattn = gres.astype(BF16)
    gattn_ref[...] = gattn
    gatt = dot_nt(gattn, wo_ref[...]).astype(BF16)
    for h in range(KVH):
        gatt_ref[h] = gatt[:, side(h)]


def turn(seq, own, got, expert_in, residual, cot, member, router, gains, wo):
    full = lambda *shape: pl.BlockSpec(shape, lambda i: (0,) * len(shape))
    mine = lambda width: pl.BlockSpec((BLK, width), lambda i: (seq, 0))
    return kernel_call(
        turn_body,
        (
            struct((KVH, BLK, LANE), BF16),
            struct((BLK, D), F32),
            struct((BLK, D), BF16),
            struct((BLK, LANE), BF16),
            struct((1, D), F32),
        ),
        flops=2 * BLK * D * D,
        nbytes=7 * 2**20,
        grid=(1,),
        in_specs=[
            full(BLK, D + LANE), full(BLK, D + LANE), full(BLK, D), full(BLK, D), mine(D), mine(LANE),
            full(D, LANE), full(8, D), full(D, D),
        ],
        out_specs=(full(KVH, BLK, LANE), full(BLK, D), full(BLK, D), full(BLK, LANE), full(1, D)),
    )(own, got, expert_in, residual, cot, member, router, gains, wo)


def finish_body(
    me_ref, rows_ref, q_ref, kv_ref, x_ref, normed_ref, gres0_ref, gres1_ref, w_ref, gains_ref, rope_ref,
    side_ref, gain0_ref, gain1_ref, grad_in_ref, keep_ref, give_ref, gq_ref, gk_ref, gw_ref,
):
    core = lax.rem(me_ref[0], 2)
    gains = gains_ref[...]
    c, s, ck, sk = rope_ref[0], rope_ref[1], rope_ref[2], rope_ref[3]
    for h in range(KVH):
        gh = rows_ref[h, :, 0:LANE].astype(F32)
        kh = rows_ref[h, :, LANE : 2 * LANE].astype(F32)
        gq_ref[:, side(h)] = gh * c - swap_halves(gh) * s
        gk_ref[:, side(h)] = kh * ck - swap_halves(kh) * sk
    q = q_ref[...]
    gq, gain_q = norm_back(q, inverse_scale(q), gains[1:2], gq_ref[...])
    gq = gq.astype(BF16)
    kv, gkv = kv_ref[...], gk_ref[...]
    r, keys = kv_scale(kv)
    weighted = jnp.where(keys, gkv * gains[2:3], 0.0)
    inner = jnp.sum(weighted * kv, axis=-1, keepdims=True) / (D // 2)
    gk = jnp.where(keys, r * weighted - kv * (r * r * r) * inner, gkv).astype(BF16)
    gain_k = jnp.sum(jnp.where(keys, gkv * kv * r, 0.0), axis=0, keepdims=True)
    normed = normed_ref[...]
    gw_ref[:, :, 0:D] = dot_tn(normed, gq).astype(BF16).reshape(N_SHARD, 64, D)
    gw_ref[:, :, D : 2 * D] = dot_tn(normed, gk).astype(BF16).reshape(N_SHARD, 64, D)
    grad = dot_nt(gq, w_ref[:, 0:D]) + dot_nt(gk, w_ref[:, D : 2 * D])
    x = x_ref[...].astype(F32)
    gx, gain_a = norm_back(x, inverse_scale(x), gains[0:1], grad)
    grad_in_ref[...] = (jnp.concatenate([gres0_ref[...], gres1_ref[...]], axis=0) + gx).astype(BF16)
    zero = jnp.zeros((2, D), F32)
    rows = jnp.concatenate([zero, gain_a, gain_q, gain_k, gain0_ref[...] + gain1_ref[...], zero], axis=0)
    which = lax.broadcasted_iota(jnp.int32, rows.shape, 0)
    place = lane_of(rows.shape) % LANE
    rows = jnp.where((which == 4) & (place >= HD), pltpu.roll(rows, HD // 2, 1), rows)
    rows = jnp.concatenate([rows, jnp.zeros((LANE - 8, D), F32)], axis=0)
    beside = (side_ref[...] + rows.T).astype(BF16)
    gw_ref[:, :, 2 * D : LAST] = beside.reshape(N_SHARD, 64, LANE)
    for k in range(PAIRS):
        keep_ref[k] = gw_ref[2 * k + core]
        give_ref[k] = gw_ref[2 * k + 1 - core]


def finish(places, rows, q, kv, x, normed, gres, first, gains, rope, beside, gain_e):
    vmem = pl.BlockSpec(memory_space=pltpu.VMEM)
    return kernel_call(
        finish_body,
        (struct((ROWS, D), BF16),) + (struct((PAIRS, 64, LAST), BF16),) * 2,
        flops=4 * 2 * ROWS * D * D,
        nbytes=15 * 2**20,
        in_specs=[pl.BlockSpec(memory_space=pltpu.SMEM)] + [vmem] * 13,
        scratch_shapes=[
            pltpu.VMEM((ROWS, D), F32),
            pltpu.VMEM((ROWS, D), F32),
            pltpu.VMEM((N_SHARD, 64, LAST), BF16),
        ],
    )(places, rows, q, kv, x, normed, *gres, first, gains, rope, beside, *gain_e)


def project_back_body(me_ref, *refs):
    att, gattn, rows, glog = refs[0:2], refs[2:4], refs[4:6], refs[6:8]
    out_ref, beside_ref = refs[9:]
    column = lax.rem(me_ref[0] // 2, 2)
    whole = dot_tn(att[0][...], gattn[0][...]) + dot_tn(att[1][...], gattn[1][...])
    whole = whole.astype(BF16).reshape(N_SHARD, 64, D)
    for z in range(4):
        for a in range(2):
            for c in range(2):
                out_ref[z, c, lax.rem(column + a, 2)] = whole[4 * z + 2 * a + c]
    beside_ref[...] = dot_tn(rows[0][...], glog[0][...]) + dot_tn(rows[1][...], glog[1][...])


def project_back(places, attended, gattn, expert_in, glog, out):
    full = lambda *shape: pl.BlockSpec(shape, lambda i: (0,) * len(shape))
    return kernel_call(
        project_back_body,
        (struct(out.shape, BF16), struct((D, LANE), F32)),
        flops=2 * ROWS * D * D,
        nbytes=6 * 2**20,
        grid=(1,),
        in_specs=[pl.BlockSpec(memory_space=pltpu.SMEM)]
        + [full(BLK, D)] * 6
        + [full(BLK, LANE)] * 2
        + [pl.BlockSpec(memory_space=pl.ANY)],
        out_specs=(
            pl.BlockSpec((4, 2, 2, 64, D), lambda i: (0, 0, 0, ROWS // 64, 0)),
            full(D, LANE),
        ),
        input_output_aliases={9: 0},
    )(places, *attended, *gattn, *expert_in, *glog, out)


def add_body(a_ref, b_ref, c_ref, d_ref, first_ref, second_ref):
    first_ref[...] = (a_ref[...].astype(F32) + b_ref[...].astype(F32)).astype(BF16)
    second_ref[...] = (c_ref[...].astype(F32) + d_ref[...].astype(F32)).astype(BF16)


def add_both(a, b, c, d):
    block = pl.BlockSpec((1,) + a.shape[1:], lambda i: (i, 0, 0))
    return kernel_call(
        add_body,
        (struct(a.shape, BF16),) * 2,
        nbytes=5 * 2**20,
        grid=(a.shape[0],),
        in_specs=[block] * 4,
        out_specs=(block,) * 2,
    )(a, b, c, d)


def prepare_body(wo_ref, wq_ref, wkv_ref, router_ref, gains_ref, out_ref):
    out_ref[:, 0:D] = wo_ref[...]
    out_ref[:, D : 2 * D] = wq_ref[...]
    low = lane_of((64, LANE)) < HD
    for pair in range(KVH // 2):
        k = wkv_ref[:, side(pair)].astype(F32)
        v = wkv_ref[:, side(pair + KVH // 2)].astype(F32)
        even = jnp.where(low, k, pltpu.roll(v, HD, 1))
        odd = jnp.where(low, pltpu.roll(k, HD, 1), v)
        at = 2 * D + 2 * pair * LANE
        out_ref[:, at : at + LANE] = even.astype(BF16)
        out_ref[:, at + LANE : at + 2 * LANE] = odd.astype(BF16)
    expert = lax.broadcasted_iota(jnp.int32, (E, LANE), 0)
    place = (lane_of((E, LANE)) == expert // 2 * 8 + expert % 2).astype(F32).astype(BF16)
    out_ref[:, SMALL : SMALL + LANE] = dot(router_ref[...], place).astype(BF16)
    column = lax.broadcasted_iota(jnp.int32, (8, LANE), 0)
    place = (lane_of((8, LANE)) == column).astype(F32).astype(BF16)
    out_ref[:, SMALL + LANE :] = dot_tn(gains_ref[...], place).astype(BF16)


def prepare(wo, wq, wkv, router, gains):
    return kernel_call(prepare_body, struct((64, SMALL + 2 * LANE), BF16), nbytes=2**20)(wo, wq, wkv, router, gains)


def interleave(kv):
    return jnp.swapaxes(kv.reshape(-1, 2, KVH, HD), 1, 2).reshape(-1, D)


def separate(kv):
    return jnp.swapaxes(kv.reshape(-1, KVH, 2, HD), 1, 2).reshape(-1, D)


def spread(per_expert):
    rows = per_expert.shape[0]
    padded = jnp.pad(per_expert.reshape(rows, N_SHARD, 2), ((0, 0), (0, 0), (0, 6)))
    return padded.reshape(rows, LANE)


def rope_tables(ctx):
    half = HD // 2
    positions = ctx * BLK + jnp.arange(BLK, dtype=jnp.int32)
    frequency = ROPE_BASE ** (-2.0 * jnp.arange(half, dtype=F32) / HD)
    angles = positions.astype(F32)[:, None] * frequency[None, :]
    c, s = jnp.cos(angles), jnp.sin(angles)
    c, s = jnp.concatenate([c, c], axis=1), jnp.concatenate([-s, s], axis=1)
    one, zero = jnp.ones_like(c), jnp.zeros_like(c)
    pairs = [(c, c), (s, s), (c, one), (s, zero)]
    tables = jnp.stack([jnp.concatenate(p, axis=1) for p in pairs])
    return jnp.concatenate([tables] * SEQS, axis=1)


def to_every(own, axis):
    count = lax.axis_size(axis)
    copies = jnp.broadcast_to(own[None], (count,) + own.shape)
    return lax.all_to_all(copies, axis, 0, 0, tiled=True)


def with_other_core(keep, give):
    got = lax.ppermute(give, "shard", OTHER_CORE)
    return (keep.astype(F32) + got.astype(F32)).astype(BF16)


def tie(*arrays):
    return lax.optimization_barrier(arrays)


def local(
    hidden_in,
    routes,
    prefix,
    gain_attention,
    w_query,
    w_keyval,
    gain_query,
    gain_key,
    w_output,
    gain_experts,
    w_router,
    w_gate_up,
    w_down,
    cotangent,
):
    shard = lax.axis_index("shard")
    ctx = lax.axis_index("ctx")
    core = shard % 2
    x = hidden_in.reshape(ROWS, D)
    cot = cotangent.reshape(ROWS, D)

    def beside(rows):
        return jnp.stack([rows, lax.ppermute(rows, "shard", X_LO)])

    def column_gather(both):
        whole = lax.all_gather(both, "shard", axis=0, axis_index_groups=COLUMNS)
        return whole.reshape((4, 2) + both.shape)

    vectors = jnp.stack([gain_attention, gain_query, jnp.pad(gain_key, (0, 32)), gain_experts])
    first = beside(prepare(w_output, w_query, w_keyval, w_router, jnp.pad(vectors, ((0, 4), (0, 0)))))

    lanes = jnp.arange(LANE, dtype=jnp.int32)
    named = jnp.where(lanes % 8 < 2, lanes // 8 * 2 + lanes % 8, -1)
    member = jnp.any(routes.reshape(ROWS, -1)[:, :, None] == named, axis=1).astype(BF16)
    sent, _ = tie(jnp.concatenate([cot, member], axis=1), first)
    sent = beside(sent)
    first = column_gather(first)

    own_w = jnp.concatenate([w_gate_up, jnp.swapaxes(w_down, 1, 2)], axis=2)
    up, down, far = (lax.ppermute(own_w, "ctx", y_shift(step)) for step in (1, -1, 2))
    own, _ = tie(own_w, sent)
    other_w = lax.ppermute(own, "ctx", X_HI)
    x, sent, other_w, up, down, far = tie(x, sent, other_w, up, down, far)
    high, low = ctx // 4 * 4, ctx % 4
    sources = []
    for step in (0, -1, 1, 2):
        sources += [high + (low + step) % 4, 4 - high + (low + step) % 4]
    places = jnp.stack([shard, *sources]).astype(jnp.int32)

    sent = column_gather(sent)
    own_member = lax.dynamic_slice(sent, (0, 0, 0, 0, D + 8 * shard), (4, 2, 2, ROWS, 2))
    own_member = own_member.reshape(N_SHARD, SEQS, BLK, 2)
    earlier = jnp.tril(jnp.ones((BLK, BLK), BF16), -1)
    slots = jnp.einsum("ts,nbse->nebt", earlier, own_member, preferred_element_type=F32)
    slots = jnp.where(jnp.transpose(own_member, (0, 3, 1, 2)) > 0, slots, -1.0)
    slots = slots.reshape(4, 2, 2, 2, ROWS)

    rope = rope_tables(ctx)
    packed, normed, q_raw, kv_raw, gains, w_whole, router = front(places, x, first, rope)
    packed = lax.all_to_all(packed, "ctx", 0, 0, tiled=True)
    def by_heads(parts):
        return lax.all_to_all(parts, "ctx", 0, 0, tiled=True)

    def to_lanes(parts):
        return lax.all_to_all(parts, "shard", 0, 0, tiled=True, axis_index_groups=LANES)

    att = by_heads(attend(prefix, packed))
    att, other_w, far_w = tie(att, other_w, far)
    other_up, other_down = (lax.ppermute(other_w, "ctx", y_shift(step)) for step in (1, -1))
    other_far = lax.ppermute(far_w, "ctx", X_HI)
    res_a, attended_a, in_a, wo = middle(0, places, x, att, first, gains)
    all_a = column_gather(beside(in_a))
    res_b, attended_b, in_b = middle(1, places, x, att, wo, gains)
    both_b, other_up, other_down, other_far, slots = tie(beside(in_b), other_up, other_down, other_far, slots)
    all_b = column_gather(both_b)

    pieces = (own_w, other_w, up, other_up, down, other_down, far, other_far)
    def column_sums(parts):
        columns = lax.psum_scatter(
            parts.reshape(PAIRS, 2 * parts.shape[3], -1),
            "shard",
            scatter_dimension=0,
            tiled=True,
            axis_index_groups=COLUMNS,
        )
        return columns.reshape(2, parts.shape[3], -1)

    def to_neighbour(rows):
        return lax.ppermute(rows, "shard", X_LO)

    common = (cot, member, router, gains, wo)
    back, *saved = experts(0, places, all_a, sent, slots, router, pieces)
    columns_a = column_sums(back)
    back, *saved = experts(1, places, all_b, sent, slots, router, pieces, saved)
    columns_b = column_sums(back)
    out, *saved = saved
    own_0, down_0, up_0, far_0 = expert_grads(0, places, *saved)
    columns_a, saved[0], far_0, down_0 = tie(columns_a, saved[0], far_0, down_0)
    got_a = to_neighbour(columns_a[1])
    far_0 = lax.ppermute(far_0, "ctx", y_shift(1))
    down_0 = lax.ppermute(down_0, "ctx", y_shift(-1))
    own_1, down_1, up_1, far_1 = expert_grads(1, places, *saved)
    got_a, far_1, up_1 = tie(got_a, far_1, up_1)
    far_1 = lax.ppermute(far_1, "ctx", y_shift(-1))
    up_1 = lax.ppermute(up_1, "ctx", y_shift(1))
    gatt_a, gres_a, gattn_a, glog_a, gain_a = turn(0, columns_a[0], got_a, in_a, res_a, *common)
    back_a = by_heads(gatt_a)
    back_a, columns_b, far_0, far_1 = tie(back_a, columns_b, far_0, far_1)
    got_b = to_neighbour(columns_b[1])
    up_0, down_1 = add_both(up_0, far_0, down_1, far_1)
    back_a, up_0, down_1 = tie(back_a, up_0, down_1)
    up_0 = lax.ppermute(up_0, "ctx", y_shift(1))
    down_1 = lax.ppermute(down_1, "ctx", y_shift(-1))
    grads_a = attend_back(0, prefix, packed, back_a)
    got_b, grads_a = tie(got_b, grads_a)
    gatt_b, gres_b, gattn_b, glog_b, gain_b = turn(1, columns_b[0], got_b, in_b, res_b, *common)
    gatt_b, gattn_b = tie(gatt_b, gattn_b)
    back_b = by_heads(gatt_b)
    out, beside_grad = project_back(
        places, (attended_a, attended_b), (gattn_a, gattn_b), (in_a, in_b), (glog_a, glog_b), out
    )
    back_b, out, up_0, down_1, up_1, down_0 = tie(back_b, out, up_0, down_1, up_1, down_0)
    columns = column_sums(out)
    grads = attend_back(1, prefix, packed, back_b, (grads_a,))
    rows = by_heads(grads)
    sums = [sum(g.astype(F32) for g in parts) for parts in ((own_0, up_0, down_0), (own_1, up_1, down_1))]
    gives = jnp.stack([g[1] for g in sums]).astype(BF16)
    gives = lax.ppermute(gives, "ctx", X_HI)
    grad_input, gw_keep, gw_give = finish(
        places, rows, q_raw, kv_raw, x, normed, (gres_a, gres_b), w_whole, gains, rope, beside_grad, (gain_a, gain_b)
    )
    gw_keep, gw_give, gives = tie(gw_keep, gw_give, gives)

    dense = with_other_core(gw_keep, gw_give).reshape(PAIRS * N_CTX, 8, -1)
    dense = lax.all_to_all(dense, ("shard", "ctx"), 0, 0, tiled=True, axis_index_groups=CHIPS)
    got = to_neighbour(columns[1, ROWS:])
    dense, g_wo, got = tie(dense, columns[0, ROWS:], got)
    g_wo = g_wo.astype(F32) + got.astype(F32)
    got = to_neighbour(columns[1, :ROWS])
    for partners in (X_HI, Y_NEAR, Y_OTHER):
        g_wo = g_wo.astype(BF16)
        g_wo = g_wo.astype(F32) + lax.ppermute(g_wo, "ctx", partners).astype(F32)
    dense = to_every(dense.astype(F32).sum(axis=0).astype(BF16), "ctx")
    dense, got, g_wo = tie(dense, got, g_wo)
    dense = dense.reshape(64, -1).astype(F32)
    beside_grad = dense[:, 2 * D :]
    g_router = beside_grad.reshape(64, N_SHARD, 8)[..., :2].reshape(64, E)
    pieces = jnp.stack([g[0] for g in sums]) + gives.astype(F32)

    moe = columns[0, :ROWS].astype(F32) + got.astype(F32)
    layer_out = (jnp.concatenate([res_a, res_b]) + moe).astype(BF16)
    return (
        layer_out.reshape(hidden_in.shape),
        grad_input.reshape(hidden_in.shape),
        beside_grad[:, 2],
        dense[:, 0:D],
        separate(dense[:, D : 2 * D]),
        beside_grad[:, 3],
        beside_grad[0:32, 4],
        g_wo,
        beside_grad[:, 5],
        g_router,
        pieces[..., : 2 * FF],
        jnp.swapaxes(pieces[..., 2 * FF :], 1, 2),
    )


def solution(mesh):
    rows = P("shard", "ctx", None)
    flat, line = P("shard", None), P("shard")
    return jax.shard_map(
        local,
        mesh=mesh,
        in_specs=(rows, rows, line, line, flat, flat, line, line, flat, line, flat, rows, P("shard", None, "ctx"), rows),
        out_specs=(rows, rows, line, flat, flat, line, line, flat, line, flat, rows, P("shard", None, "ctx")),
        check_vma=False,
    )
```
